32 devices in a mesh: bearing: 8 (over z, x), freq: 4 (over y, core).
Axes of the slice: x: 2, y: 2, z: 4, core: 2. Of those that a mesh axis runs over, the one named last changes fastest.
Arguments:
- starter: bfloat16 [4, 2, 256, 1024], P('freq', None, 'bearing'), may hold values from -6 to 6
- propagator: bfloat16 [4, 2, 1024, 1024], P('freq'), may hold values from -1 to 1
- wavenumber: float32 [4], P('freq'), may hold values from 0.5 to 2
- sediment_loss: float32 [4], P('freq'), may hold values from 0.1 to 1
- env_speed: bfloat16 [256, 1024], P('bearing'), may hold values from -6 to 6
- bottom: int32 [256], P('bearing'), may hold values from 256 to 1023
- track_column: int32 [256, 24], P('bearing'), may hold values from 0 to 255
Outputs:
- band_power: float32 [256, 128], P(('bearing', 'freq'))
The draws below stay inside these ranges and needn't reach their ends.
All inputs are finite; a program needn't handle non-finite values.
Results may differ from the reference program's by a relative error of at most 0.0011.
Values may be sent and summed in bfloat16 or wider, within the bound.
No kernel may reach another device: no remote copies, remote signals or barrier semaphores. Data moves between devices by JAX's collectives and lax.ppermute only.
A program may use at most 64 MiB of HBM per device.

```python
import math
import jax
import jax.numpy as jnp
import numpy as np
from jax import lax

NZ = 1024
BAND_CELLS = 8
STEPS = 24
BANDS = 128
BEARINGS = 256
FREQS = 4
COLS = 256


def draw_propagator(key, part):
    key = jax.random.fold_in(key, 11)
    key_phase, key_turn, key_global, key_noise = jax.random.split(key, 4)
    cells = jnp.arange(NZ, dtype=jnp.int32) + 1
    product = cells[:, None] * cells[None, :] % (2 * (NZ + 1))
    sine_table = math.sqrt(2.0 / (NZ + 1)) * jnp.sin(product.astype(jnp.float32) * (math.pi / (NZ + 1)))
    angles = jax.random.uniform(key_phase, (FREQS, NZ), jnp.float32, -math.pi, math.pi)
    offsets = angles[:, :, None] - angles[:, None, :]
    turn = jax.random.uniform(key_turn, (FREQS, 1, 1), jnp.float32, 0.5, 1.0)
    noise = jax.random.normal(key_noise, (FREQS, 2, NZ, NZ), jnp.float32)
    overall = jax.random.uniform(key_global, (FREQS, 1, 1), jnp.float32, -math.pi, math.pi)
    identity = jnp.eye(NZ, dtype=jnp.float32)[None]
    inner_re = jnp.cos(turn) * identity - jnp.sin(turn) * jnp.sin(offsets) * sine_table[None]
    inner_im = jnp.sin(turn) * jnp.cos(offsets) * sine_table[None]
    outer_re = jnp.cos(overall) * inner_re - jnp.sin(overall) * inner_im
    outer_im = jnp.sin(overall) * inner_re + jnp.cos(overall) * inner_im
    spread = 0.15 / math.sqrt(2.0 * NZ)
    matrix = (jnp.stack([outer_re, outer_im], axis=1) + noise * spread) / math.sqrt(1.0 + 0.15 * 0.15)
    return matrix.astype(jnp.bfloat16)


def with_ends(array, stream_key, smallest, largest):
    index_at = [jax.random.randint(jax.random.fold_in(stream_key, axis), (), 0, length) for axis, length in enumerate(array.shape)]
    main_axis = array.shape.index(max(array.shape))
    next_to = index_at[:main_axis] + [(index_at[main_axis] + 1) % array.shape[main_axis]] + index_at[main_axis + 1:]
    return array.at[tuple(index_at)].set(smallest).at[tuple(next_to)].set(largest)


def level_of(key, dims, pieces, smallest, top_value):
    def one(axis_at, blocks):
        draws = jax.random.uniform(jax.random.fold_in(jax.random.fold_in(key, 6), axis_at), (blocks,), jnp.float32, smallest / len(pieces), top_value / len(pieces))
        return jnp.repeat(jnp.exp(draws), dims[axis_at] // blocks).reshape((-1,) + (1,) * (len(dims) - axis_at - 1))

    gain = one(*pieces[0])
    for cut in pieces[1:]:
        gain = gain * one(*cut)
    return gain


def rank_bounds(number_of, skew):
    weights = [(1 << 20) // math.isqrt(grade ** skew) + 1 for grade in range(1, number_of + 1)]
    scale = 1 + sum(weights) // (1 << 30)
    return np.cumsum(np.array([max(1, weight // scale) for weight in weights]))


def skewed_ids(rng, extent, amount, slope):
    listing = rank_bounds(amount, slope)
    ticket = jax.random.randint(jax.random.fold_in(rng, 1), extent, 0, int(listing[amount - 1]))
    standing = jnp.searchsorted(jnp.asarray(listing, jnp.int32), ticket, side="right")
    return jax.random.permutation(jax.random.fold_in(rng, 2), amount)[standing].astype(jnp.int32)


def bell_draw(own_key, shape, width, most, cuts=(), kind=jnp.bfloat16):
    factor_of = level_of(own_key, shape, cuts, -0.22, 0.18) if cuts else 1.0
    array = jax.random.normal(own_key, shape, jnp.float32) * width * factor_of
    return jnp.minimum(jnp.maximum(array, -most), most).astype(kind)


def setup_inputs(seed: int = 0) -> dict:
    key_of = jax.random.split(jax.random.key(seed), 8)
    starter = bell_draw(key_of[0], (FREQS, 2, BEARINGS, NZ), 1.0, 6.0, ((0, 4), (2, 8)))
    propagator = draw_propagator(jax.random.fold_in(key_of[7], 71), 0)
    wavenumber = jnp.clip(jnp.exp(math.log(2.0) - 1.3862944 * jax.random.uniform(key_of[2], (FREQS,), jnp.float32) ** level_of(key_of[2], (FREQS,), ((0, 4),), -0.2, 0.2)), 0.5, 2.0)
    sediment_loss = jnp.clip(jnp.exp(math.log(1.0) - 2.3025851 * jax.random.uniform(key_of[3], (FREQS,), jnp.float32) ** level_of(key_of[3], (FREQS,), ((0, 4),), -0.2, 0.2)), 0.1, 1.0)
    env_speed = bell_draw(key_of[4], (COLS, NZ), 1.0, 6.0, ((0, 8),))
    bottom = with_ends(jax.random.randint(key_of[5], (COLS,), NZ // 4, NZ), jax.random.fold_in(key_of[5], 1), NZ // 4, NZ - 1).astype(jnp.int32)
    track_column = with_ends(skewed_ids(key_of[6], (BEARINGS, STEPS), COLS, 1), jax.random.fold_in(key_of[6], 3), 0, COLS - 1).astype(jnp.int32)
    return {"starter": starter, "propagator": propagator, "wavenumber": wavenumber, "sediment_loss": sediment_loss, "env_speed": env_speed, "bottom": bottom, "track_column": track_column}


def reference(starter, propagator, wavenumber, sediment_loss, env_speed, bottom, track_column):
    depth_index = jnp.arange(NZ, dtype=jnp.int32)
    prop_re = propagator[:, 0].astype(jnp.float32)
    prop_im = propagator[:, 1].astype(jnp.float32)
    decay = jnp.exp(-sediment_loss)[:, None, None]

    def advance(carried, columns):
        stacked = carried.astype(jnp.float32)
        mixed_re = jnp.einsum('fbz,fzy->fby', stacked, prop_re, precision=lax.Precision.HIGHEST)
        mixed_im = jnp.einsum('fbz,fzy->fby', stacked, prop_im, precision=lax.Precision.HIGHEST)
        moved_re = mixed_re[:, :BEARINGS] - mixed_im[:, BEARINGS:]
        moved_im = mixed_im[:, :BEARINGS] + mixed_re[:, BEARINGS:]
        sounds = env_speed[columns].astype(jnp.float32)
        phases = wavenumber[:, None, None] * sounds[None]
        deep_cells = depth_index[None, :] >= bottom[columns][:, None]
        damping = jnp.where(deep_cells[None], decay, jnp.float32(1.0))
        cosine = jnp.cos(phases)
        sine = jnp.sin(phases)
        screened_re = (moved_re * cosine - moved_im * sine) * damping
        screened_im = (moved_re * sine + moved_im * cosine) * damping
        squared = screened_re * screened_re + screened_im * screened_im
        powers = squared.reshape(FREQS, BEARINGS, BANDS, BAND_CELLS).sum(-1).sum(0)
        following = jnp.concatenate([screened_re, screened_im], axis=1).astype(jnp.bfloat16)
        return following, powers

    initial = starter.reshape(FREQS, 2 * BEARINGS, NZ)
    final_field, powers = lax.scan(advance, initial, track_column.T)
    targets = track_column.T.reshape(-1).astype(jnp.int32)
    grid = jnp.zeros((COLS, BANDS), jnp.float32).at[targets].add(powers.reshape(-1, BANDS))
    return grid * (COLS / (BEARINGS * STEPS * FREQS))
```

```python
import functools

import jax
import jax.numpy as jnp
from jax import lax
from jax.experimental import pallas as pl
from jax.experimental.pallas import tpu as pltpu
from jax.sharding import PartitionSpec as P

BAND_CELLS = 8
LANES = 128
CHUNK = 256
QUARTER_TURN = 0.6366197723675814
SIN_TERMS = (1.5707963219600276, -0.6459634781534198, 0.079680222858126, -0.004602163104811149)
COS_TERMS = (0.9999999723759501, -1.2336970108360321, 0.25359860771245774, -0.020408255467132635)


def polynomial(terms, square):
    total = jnp.float32(terms[-1])
    for term in terms[-2::-1]:
        total = total * square + jnp.float32(term)
    return total


def sine_and_cosine(turns):
    nearest = jnp.round(turns)
    rest = turns - nearest
    quadrant = nearest.astype(jnp.int32)
    square = rest * rest
    sine = polynomial(SIN_TERMS, square) * rest
    cosine = polynomial(COS_TERMS, square)
    odd = (quadrant & 1) != 0
    return (
        jnp.where(odd, cosine, sine),
        jnp.where(odd, sine, cosine),
        (quadrant & 2) != 0,
        ((quadrant + 1) & 2) != 0,
    )


def propagate(
    bands_of,
    track_smem, bottom_smem, scalars_smem, ids_ref, starter_ref, prop_ref, *rest,
):
    env_refs, (grid_ref, table, field_a, field_b, sin_a, cos_a, sin_b, cos_b, powers) = rest[:-9], rest[-9:]
    owner_total = len(env_refs)
    columns_here, depth_cells = env_refs[0].shape
    pieces = depth_cells // LANES
    steps, bearings = track_smem.shape
    column_total = grid_ref.shape[0]
    me = scalars_smem[2].astype(jnp.int32)
    per_turn = scalars_smem[0] * jnp.float32(QUARTER_TURN)
    decay = scalars_smem[1]

    for shift, env_ref in enumerate(env_refs):
        owner = lax.rem(me - shift + owner_total, owner_total)
        base = owner * (columns_here * pieces)
        for piece in range(pieces):
            block = env_ref[:, piece * LANES : (piece + 1) * LANES].astype(jnp.float32)
            table[pl.ds(base + piece, columns_here, stride=pieces), :] = block * per_turn
    field_a[...] = starter_ref[...]

    depth_index = lax.broadcasted_iota(jnp.int32, (pieces, LANES), 0) * LANES + lax.broadcasted_iota(
        jnp.int32, (pieces, LANES), 1
    )

    def prepare(step, sin_ref, cos_ref):
        for bearing in range(bearings):
            column = track_smem[step, bearing]
            turns = table[pl.ds(pl.multiple_of(column * pieces, pieces), pieces), :]
            sine, cosine, sine_minus, cosine_minus = sine_and_cosine(turns)
            damping = jnp.where(depth_index >= bottom_smem[column], decay, jnp.float32(1.0))
            rows = slice(bearing * pieces, (bearing + 1) * pieces)
            sin_ref[rows, :] = sine * jnp.where(sine_minus, -damping, damping)
            cos_ref[rows, :] = cosine * jnp.where(cosine_minus, -damping, damping)

    lane = lax.broadcasted_iota(jnp.int32, (bearings, LANES), 1)

    def fold(first, second, width):
        return jnp.where(
            (lane & width) == 0,
            first + pltpu.roll(first, LANES - width, 1),
            second + pltpu.roll(second, width, 1),
        )

    def advance(step, field, following, sin_ref, cos_ref):
        squares = []
        for start in range(0, depth_cells, CHUNK):
            cells = slice(start, start + CHUNK)
            mixed_re = jnp.dot(field[...], prop_ref[0, :, cells], preferred_element_type=jnp.float32)
            mixed_im = jnp.dot(field[...], prop_ref[1, :, cells], preferred_element_type=jnp.float32)
            moved_re = mixed_re[:bearings] - mixed_im[bearings:]
            moved_im = mixed_im[:bearings] + mixed_re[bearings:]
            for part in range(CHUNK // LANES):
                piece = start // LANES + part
                inner = slice(part * LANES, (part + 1) * LANES)
                outer = slice(piece * LANES, (piece + 1) * LANES)
                sine = sin_ref[pl.ds(piece, bearings, stride=pieces), :]
                cosine = cos_ref[pl.ds(piece, bearings, stride=pieces), :]
                screened_re = moved_re[:, inner] * cosine - moved_im[:, inner] * sine
                screened_im = moved_re[:, inner] * sine + moved_im[:, inner] * cosine
                following[:bearings, outer] = screened_re.astype(jnp.bfloat16)
                following[bearings:, outer] = screened_im.astype(jnp.bfloat16)
                squares.append(screened_re * screened_re + screened_im * screened_im)
        width = 1
        while len(squares) > 1:
            squares = [fold(squares[i], squares[i + 1], width) for i in range(0, len(squares), 2)]
            width *= 2
        rows = pl.ds(pl.multiple_of(step * bearings, bearings), bearings)
        powers[rows, :] = squares[0]

    prepare(0, sin_a, cos_a)

    def two_steps(pair, carry):
        step = pair * 2
        prepare(step + 1, sin_b, cos_b)
        advance(step, field_a, field_b, sin_a, cos_a)
        prepare(jnp.minimum(step + 2, steps - 1), sin_a, cos_a)
        advance(step + 1, field_b, field_a, sin_b, cos_b)
        return carry

    lax.fori_loop(0, steps // 2, two_steps, 0)

    tracks = steps * bearings
    chosen = (lax.broadcasted_iota(jnp.int32, (column_total, tracks), 0) == ids_ref[...]).astype(jnp.bfloat16)
    high = powers[...].astype(jnp.bfloat16)
    low = (powers[...] - high.astype(jnp.float32)).astype(jnp.bfloat16)
    both = jnp.dot(chosen, jnp.concatenate([high, low], axis=1), preferred_element_type=jnp.float32)
    grid_ref[...] = both[:, :LANES] + both[:, LANES:]


def finish(scale, parts_ref, out_ref):
    total = jnp.sum(parts_ref[...].astype(jnp.float32), axis=0) * jnp.float32(scale)
    row = lax.broadcasted_iota(jnp.int32, (LANES, LANES), 0)
    column = lax.broadcasted_iota(jnp.int32, (LANES, LANES), 1)
    groups = LANES // BAND_CELLS
    place = (row % BAND_CELLS) * groups + row // BAND_CELLS
    order = (place == column).astype(jnp.float32)
    out_ref[...] = jnp.dot(total, order, precision=lax.Precision.HIGHEST, preferred_element_type=jnp.float32)


def on_device(starter, propagator, wavenumber, sediment_loss, env_speed, bottom, track_column):
    bearings_here, steps = track_column.shape
    columns_here, depth_cells = env_speed.shape
    bands = depth_cells // BAND_CELLS
    owners = lax.axis_size("bearing")
    devices = owners * lax.axis_size("freq")
    column_total = columns_here * owners

    blocks = [env_speed] + [
        lax.ppermute(env_speed, "bearing", [(i, (i + shift) % owners) for i in range(owners)])
        for shift in range(1, owners)
    ]
    bottoms_all = lax.all_gather(bottom, "bearing", axis=0, tiled=True)
    tracks = track_column.T
    scalars = jnp.stack(
        [wavenumber[0], jnp.exp(-sediment_loss[0]), lax.axis_index("bearing").astype(jnp.float32)]
    )
    pieces = depth_cells // LANES
    smem = pl.BlockSpec(memory_space=pltpu.SMEM)
    vmem = pl.BlockSpec(memory_space=pltpu.VMEM)
    grid = pl.pallas_call(
        functools.partial(propagate, bands),
        out_shape=jax.ShapeDtypeStruct((column_total, bands), jnp.float32),
        in_specs=[smem] * 3 + [vmem] * (3 + len(blocks)),
        out_specs=vmem,
        scratch_shapes=[
            pltpu.VMEM((column_total * pieces, LANES), jnp.float32),
            pltpu.VMEM((2 * bearings_here, depth_cells), jnp.bfloat16),
            pltpu.VMEM((2 * bearings_here, depth_cells), jnp.bfloat16),
        ]
        + [pltpu.VMEM((bearings_here * pieces, LANES), jnp.float32)] * 4
        + [pltpu.VMEM((steps * bearings_here, bands), jnp.float32)],
        compiler_params=pltpu.CompilerParams(vmem_limit_bytes=40 * 1024 * 1024),
        name="propagate",
    )(
        tracks, bottoms_all, scalars, tracks.reshape(1, -1),
        starter[0].reshape(2 * bearings_here, depth_cells), propagator[0], *blocks,
    )
    parts = lax.all_to_all(
        grid.reshape(devices, column_total // devices, bands), ("bearing", "freq"), 0, 0
    )
    scale = column_total / (bearings_here * owners * steps * lax.axis_size("freq"))
    return pl.pallas_call(
        functools.partial(finish, scale),
        out_shape=jax.ShapeDtypeStruct((column_total // devices, bands), jnp.float32),
        in_specs=[vmem],
        out_specs=vmem,
        name="finish",
    )(parts)


def solution(mesh):
    in_specs = (
        P("freq", None, "bearing", None),
        P("freq", None, None, None),
        P("freq"),
        P("freq"),
        P("bearing", None),
        P("bearing"),
        P("bearing", None),
    )
    out_specs = P(("bearing", "freq"), None)
    return jax.shard_map(
        on_device, mesh=mesh, in_specs=in_specs, out_specs=out_specs, check_vma=False
    )
```

```python
import functools

import jax
import jax.numpy as jnp
from jax import lax
from jax.experimental import pallas as pl
from jax.experimental.pallas import tpu as pltpu
from jax.sharding import PartitionSpec as P

BAND_CELLS = 8
LANES = 128
TILE = 256
PAD_ROWS = 64
EXTRA_ROWS = 16
CODE_BASE = 256
QUARTER_TURN = 0.6366197723675814
SIN_TERMS = (1.5707963219600276, -0.6459634781534198, 0.079680222858126, -0.004602163104811149)
COS_TERMS = (0.9999999723759501, -1.2336970108360321, 0.25359860771245774, -0.020408255467132635)
VMEM_LIMIT = 60 * 1024 * 1024


def polynomial(terms, square):
    total = jnp.float32(terms[-1])
    for term in terms[-2::-1]:
        total = total * square + jnp.float32(term)
    return total


def sine_and_cosine(turns):
    nearest = jnp.round(turns)
    rest = turns - nearest
    quadrant = nearest.astype(jnp.int32)
    square = rest * rest
    sine = polynomial(SIN_TERMS, square) * rest
    cosine = polynomial(COS_TERMS, square)
    odd = (quadrant & 1) != 0
    return (
        jnp.where(odd, cosine, sine),
        jnp.where(odd, sine, cosine),
        (quadrant & 2) != 0,
        ((quadrant + 1) & 2) != 0,
    )


def pack(env_ref, bottom_ref, out_ref, wide):
    columns, depth_cells = env_ref.shape
    pieces = depth_cells // LANES
    for piece in range(pieces):
        block = env_ref[:, piece * LANES : (piece + 1) * LANES].astype(jnp.float32)
        wide[pl.ds(piece, columns, stride=pieces), :] = block
    rows = columns * pieces
    out_ref[:rows, :] = wide[...].astype(jnp.bfloat16)
    bottom = jnp.concatenate([bottom_ref[...], jnp.zeros((1, LANES - columns), jnp.int32)], axis=1)
    row = lax.broadcasted_iota(jnp.int32, (EXTRA_ROWS, LANES), 0)
    high = lax.shift_right_logical(bottom, 8)
    extra = jnp.where(row == 0, high, jnp.where(row == 1, bottom & (CODE_BASE - 1), 0))
    out_ref[rows:, :] = extra.astype(jnp.float32).astype(jnp.bfloat16)


def propagate(
    track_smem, place_smem, scalars_smem, tracks_ref, starter_ref, prop_ref, own_ref, direct_ref, passed_ref,
    grid_ref, prop, prop_sems, table, bottom_vmem, bottom_smem, bottom_sem,
    field_a, field_b, sin_a, cos_a, sin_b, cos_b, powers,
):
    pieces, double_depth, _ = prop.shape
    depth_cells = double_depth // 2
    steps, bearings = track_smem.shape
    column_total = grid_ref.shape[0]
    block_rows = own_ref.shape[0]
    cell_rows = block_rows - EXTRA_ROWS
    columns_here = cell_rows // pieces
    rounds = direct_ref.shape[0] // block_rows
    per_turn = scalars_smem[0] * jnp.float32(QUARTER_TURN)
    decay = scalars_smem[1]

    loads = [
        pltpu.make_async_copy(
            prop_ref.at[:, piece * LANES : (piece + 1) * LANES], prop.at[piece], prop_sems.at[piece]
        )
        for piece in range(pieces)
    ]
    for load in loads:
        load.start()

    blocks = [own_ref[...]]
    for ref in (direct_ref, passed_ref):
        blocks += [ref[turn * block_rows : (turn + 1) * block_rows, :] for turn in range(rounds)]
    for index, block in enumerate(blocks):
        codes = block[cell_rows:, :].astype(jnp.float32)
        bottom = codes[0:1] * jnp.float32(CODE_BASE) + codes[1:2]
        bottom_vmem[pl.ds(place_smem[index], 1), :] = bottom.astype(jnp.int32)
    to_smem = pltpu.make_async_copy(bottom_vmem, bottom_smem, bottom_sem)
    to_smem.start()
    for index, block in enumerate(blocks):
        rows = pl.ds(pl.multiple_of(place_smem[index] * cell_rows, cell_rows), cell_rows)
        table[rows, :] = block[:cell_rows, :].astype(jnp.float32) * per_turn

    def put(field, cells, real, imaginary):
        beyond = slice(depth_cells + cells.start, depth_cells + cells.stop)
        field[:bearings, cells] = real
        field[:bearings, beyond] = -imaginary
        field[bearings:, cells] = imaginary
        field[bearings:, beyond] = real

    put(field_a, slice(0, depth_cells), starter_ref[:bearings, :], starter_ref[bearings:, :])

    depth_index = lax.broadcasted_iota(jnp.int32, (pieces, LANES), 0) * LANES + lax.broadcasted_iota(
        jnp.int32, (pieces, LANES), 1
    )

    def prepare(step, sin_ref, cos_ref, which):
        for bearing in which:
            column = track_smem[step, bearing]
            owner = lax.div(column, columns_here)
            bottom = bottom_smem[owner, column - owner * columns_here]
            turns = table[pl.ds(pl.multiple_of(column * pieces, pieces), pieces), :]
            sine, cosine, sine_minus, cosine_minus = sine_and_cosine(turns)
            damping = jnp.where(depth_index >= bottom, decay, jnp.float32(1.0))
            rows = slice(bearing * pieces, (bearing + 1) * pieces)
            sin_ref[rows, :] = sine * jnp.where(sine_minus, -damping, damping)
            cos_ref[rows, :] = cosine * jnp.where(cosine_minus, -damping, damping)

    lane = lax.broadcasted_iota(jnp.int32, (bearings, LANES), 1)

    def fold(first, second, width):
        return jnp.where(
            (lane & width) == 0,
            first + pltpu.roll(first, LANES - width, 1),
            second + pltpu.roll(second, width, 1),
        )

    tiles = depth_cells // TILE
    halves = tiles // 2
    pieces_in = 2 * TILE // LANES
    early = [tile + part * tiles for tile in range(tiles - 2) for part in range(2)]
    late = [tile + part * tiles for tile in range(tiles - 2, tiles) for part in range(2)]
    slots_of_step = halves * (len(early) + len(late))
    nothing = jnp.zeros((PAD_ROWS, TILE), jnp.bfloat16)

    def run(*accumulators):
        sums, spare = accumulators[: 2 * halves], accumulators[2 * halves :]
        count = [0]

        def multiply(field, half, tile):
            register = count[0] % 2
            count[0] += 1
            cells = slice(tile * TILE, (tile + 1) * TILE)
            for unit in range(2):
                first = (2 * half + unit) * (TILE // LANES)
                weights = jnp.concatenate([prop[first, cells, :], prop[first + 1, cells, :]], axis=1)
                pltpu.matmul_push_rhs(weights, register, unit)
            for unit in range(2):
                pltpu.matmul_acc_lhs(sums[2 * half + unit], field[:, cells], load_staged_rhs=register)
                pltpu.matmul_acc_lhs(spare[unit], nothing)

        def begin(field):
            for half in range(halves):
                for tile in early:
                    multiply(field, half, tile)

        def advance(step, field, following, sin_ref, cos_ref, next_sin, next_cos):
            work = [[] for _ in range(slots_of_step + 1)]
            share = -(-bearings // slots_of_step)
            coming = jnp.minimum(step + 1, steps - 1)
            for slot in range(slots_of_step):
                which = range(slot * share, min(bearings, (slot + 1) * share))
                work[slot].append(functools.partial(prepare, coming, next_sin, next_cos, which))
            moved = {}
            folded = {}

            def pop(half):
                for unit in range(2):
                    moved[2 * half + unit] = pltpu.matmul_pop(sums[2 * half + unit])

            def screen(piece):
                value = moved[piece * LANES // TILE]
                inner = slice(piece * LANES % TILE, piece * LANES % TILE + LANES)
                moved_re = value[:bearings, inner]
                moved_im = value[bearings:, inner]
                sine = sin_ref[pl.ds(piece, bearings, stride=pieces), :]
                cosine = cos_ref[pl.ds(piece, bearings, stride=pieces), :]
                screened_re = moved_re * cosine - moved_im * sine
                screened_im = moved_re * sine + moved_im * cosine
                outer = slice(piece * LANES, (piece + 1) * LANES)
                put(following, outer, screened_re.astype(jnp.bfloat16), screened_im.astype(jnp.bfloat16))
                level, value = 1, screened_re * screened_re + screened_im * screened_im
                at = piece
                while at % 2 == 1:
                    value = fold(folded.pop((level, at - 1)), value, level)
                    at //= 2
                    level *= 2
                folded[level, at] = value

            for half in range(halves):
                after = (half + 1) * len(late)
                work[after].append(functools.partial(pop, half))
                for index in range(pieces_in):
                    slot = after + 1 + index
                    if half < halves - 1:
                        slot = min(slot, after + len(late) - 1)
                    work[min(slot, slots_of_step)].append(functools.partial(screen, half * pieces_in + index))
            slot = 0
            for source, order in ((field, late), (following, early)):
                for half in range(halves):
                    for tile in order:
                        multiply(source, half, tile)
                        for item in work[slot]:
                            item()
                        slot += 1
            for item in work[slot]:
                item()
            rows = pl.ds(pl.multiple_of(step * bearings, bearings), bearings)
            powers[rows, :] = folded[pieces, 0]

        for load in loads:
            load.wait()
        begin(field_a)
        to_smem.wait()
        prepare(0, sin_a, cos_a, range(bearings))

        def two_steps(pair, carry):
            advance(pair * 2, field_a, field_b, sin_a, cos_a, sin_b, cos_b)
            advance(pair * 2 + 1, field_b, field_a, sin_b, cos_b, sin_a, cos_a)
            return carry

        lax.fori_loop(0, steps // 2, two_steps, 0)
        for accumulator in accumulators:
            pltpu.matmul_pop(accumulator)

    pl.run_scoped(
        run,
        *[pltpu.ACC(unit % 2)((2 * bearings, TILE), jnp.float32) for unit in range(2 * halves)],
        *[pltpu.ACC(unit)((PAD_ROWS, TILE), jnp.float32) for unit in range(2)],
    )

    group = TILE // bearings
    lanes_of_row = lax.broadcasted_iota(jnp.int32, (1, LANES), 1)

    def ids_of(first):
        parts = []
        for start in range(first, first + group, LANES // bearings):
            row = tracks_ref[start : start + 1, :]
            total = jnp.concatenate([row, jnp.zeros((1, LANES - bearings), jnp.int32)], axis=1)
            for index in range(1, LANES // bearings):
                row = tracks_ref[start + index : start + index + 1, :]
                row = jnp.concatenate([row, jnp.zeros((1, LANES - bearings), jnp.int32)], axis=1)
                total = total + pltpu.roll(row, index * bearings, 1)
            parts.append(total)
        return jnp.concatenate(parts, axis=1)

    half_columns = column_total // 2

    def scatter(*sums):
        for index, start in enumerate(range(0, steps, group)):
            ids = ids_of(start)
            value = powers[start * bearings : (start + group) * bearings, :]
            high = value.astype(jnp.bfloat16)
            low = (value - high.astype(jnp.float32)).astype(jnp.bfloat16)
            both = jnp.concatenate([high, low], axis=1)
            for unit in range(2):
                pltpu.matmul_push_rhs(both, index % 2, unit)
            for unit in range(2):
                column = lax.broadcasted_iota(jnp.int32, (half_columns, TILE), 0) + unit * half_columns
                chosen = (column == ids).astype(jnp.bfloat16)
                pltpu.matmul_acc_lhs(sums[unit], chosen, load_staged_rhs=index % 2)
        for unit in range(2):
            total = pltpu.matmul_pop(sums[unit])
            grid_ref[unit * half_columns : (unit + 1) * half_columns, :] = total[:, :LANES] + total[:, LANES:]

    pl.run_scoped(scatter, *[pltpu.ACC(unit)((half_columns, TILE), jnp.float32) for unit in range(2)])


def finish(scale, parts_ref, out_ref):
    total = jnp.sum(parts_ref[...].astype(jnp.float32), axis=0) * jnp.float32(scale)
    row = lax.broadcasted_iota(jnp.int32, (LANES, LANES), 0)
    column = lax.broadcasted_iota(jnp.int32, (LANES, LANES), 1)
    groups = LANES // BAND_CELLS
    place = (row % BAND_CELLS) * groups + row // BAND_CELLS
    order = (place == column).astype(jnp.float32)
    out_ref[...] = jnp.dot(total, order, precision=lax.Precision.HIGHEST, preferred_element_type=jnp.float32)


def on_device(starter, propagator, wavenumber, sediment_loss, env_speed, bottom, track_column):
    bearings_here, steps = track_column.shape
    columns_here, depth_cells = env_speed.shape
    bands = depth_cells // BAND_CELLS
    owners = lax.axis_size("bearing")
    freqs = lax.axis_size("freq")
    devices = owners * freqs
    column_total = columns_here * owners
    pieces = depth_cells // LANES
    smem = pl.BlockSpec(memory_space=pltpu.SMEM)
    vmem = pl.BlockSpec(memory_space=pltpu.VMEM)

    own = pl.pallas_call(
        pack,
        out_shape=jax.ShapeDtypeStruct((columns_here * pieces + EXTRA_ROWS, LANES), jnp.bfloat16),
        in_specs=[vmem] * 2,
        out_specs=vmem,
        scratch_shapes=[pltpu.VMEM((columns_here * pieces, LANES), jnp.float32)],
        name="pack",
    )(env_speed, bottom.reshape(1, -1))

    turns = [(offset, offset - 1) for offset in range(owners - 1, 0, -2)]
    received = []
    for turn in turns:
        pairs = [
            (bearing * freqs + freq, (bearing ^ turn[freq % 2]) * freqs + freq)
            for bearing in range(owners)
            for freq in range(freqs)
            if turn[freq % 2]
        ]
        received.append(lax.ppermute(own, ("bearing", "freq"), pairs))
    direct = jnp.concatenate(received, axis=0)
    passed = lax.ppermute(direct, "freq", [(freq, freq ^ 1) for freq in range(freqs)])

    me = lax.axis_index("bearing")
    core = lax.axis_index("freq") % 2
    offsets = jnp.asarray([[0] + [turn[unit] for unit in order for turn in turns] for order in ((0, 1), (1, 0))], jnp.int32)
    mine = lax.dynamic_index_in_dim(offsets, core, 0, keepdims=False)
    places = jnp.where((mine == 0) & (jnp.arange(mine.shape[0]) > 0), owners, me ^ mine)
    scalars = jnp.stack([wavenumber[0], jnp.exp(-sediment_loss[0])])
    tracks = track_column.T
    grid = pl.pallas_call(
        propagate,
        out_shape=jax.ShapeDtypeStruct((column_total, bands), jnp.float32),
        in_specs=[smem] * 3 + [vmem] * 2 + [pl.BlockSpec(memory_space=pl.ANY)] + [vmem] * 3,
        out_specs=vmem,
        scratch_shapes=[
            pltpu.VMEM((pieces, 2 * depth_cells, LANES), jnp.bfloat16),
            pltpu.SemaphoreType.DMA((pieces,)),
            pltpu.VMEM(((owners + 1) * columns_here * pieces, LANES), jnp.float32),
            pltpu.VMEM((owners + 8, LANES), jnp.int32),
            pltpu.SMEM((owners + 8, LANES), jnp.int32),
            pltpu.SemaphoreType.DMA,
        ]
        + [pltpu.VMEM((2 * bearings_here, 2 * depth_cells), jnp.bfloat16)] * 2
        + [pltpu.VMEM((bearings_here * pieces, LANES), jnp.float32)] * 4
        + [pltpu.VMEM((steps * bearings_here, bands), jnp.float32)],
        compiler_params=pltpu.CompilerParams(vmem_limit_bytes=VMEM_LIMIT),
        name="propagate",
    )(
        tracks, places, scalars, tracks, starter[0].reshape(2 * bearings_here, depth_cells),
        propagator[0].reshape(2 * depth_cells, depth_cells), own, direct, passed,
    )
    parts = lax.all_to_all(
        grid.reshape(devices, column_total // devices, bands), ("bearing", "freq"), 0, 0
    )
    scale = column_total / (bearings_here * owners * steps * freqs)
    return pl.pallas_call(
        functools.partial(finish, scale),
        out_shape=jax.ShapeDtypeStruct((column_total // devices, bands), jnp.float32),
        in_specs=[vmem],
        out_specs=vmem,
        name="finish",
    )(parts)


def solution(mesh):
    in_specs = (
        P("freq", None, "bearing", None),
        P("freq", None, None, None),
        P("freq"),
        P("freq"),
        P("bearing", None),
        P("bearing"),
        P("bearing", None),
    )
    out_specs = P(("bearing", "freq"), None)
    mapped = jax.shard_map(
        on_device, mesh=mesh, in_specs=in_specs, out_specs=out_specs, check_vma=False
    )

    def program(*arrays):
        with jax.sharding.use_abstract_mesh(mesh.abstract_mesh):
            return mapped(*arrays)

    return program
```

```python
import functools

import jax
import jax.numpy as jnp
from jax import lax
from jax.experimental import pallas as pl
from jax.experimental.pallas import tpu as pltpu
from jax.sharding import PartitionSpec as P

BAND_CELLS = 8
LANES = 128
TILE = 256
PAD_ROWS = 64
EXTRA_ROWS = 16
CODE_BASE = 256
QUARTER_TURN = 0.6366197723675814
SIN_TERMS = (1.5707963219600276, -0.6459634781534198, 0.079680222858126, -0.004602163104811149)
COS_TERMS = (0.9999999723759501, -1.2336970108360321, 0.25359860771245774, -0.020408255467132635)
VMEM_LIMIT = 24 * 1024 * 1024
SPREAD_LIMIT = 24 * 1024 * 1024


def polynomial(terms, square):
    total = jnp.float32(terms[-1])
    for term in terms[-2::-1]:
        total = total * square + jnp.float32(term)
    return total


def sine_and_cosine(turns):
    nearest = jnp.round(turns)
    rest = turns - nearest
    quadrant = nearest.astype(jnp.int32)
    square = rest * rest
    sine = polynomial(SIN_TERMS, square) * rest
    cosine = polynomial(COS_TERMS, square)
    odd = (quadrant & 1) != 0
    return (
        jnp.where(odd, cosine, sine),
        jnp.where(odd, sine, cosine),
        (quadrant & 2) != 0,
        ((quadrant + 1) & 2) != 0,
    )


def pack(env_ref, bottom_ref, out_ref, wide):
    columns, depth_cells = env_ref.shape
    pieces = depth_cells // LANES
    for piece in range(pieces):
        block = env_ref[:, piece * LANES : (piece + 1) * LANES].astype(jnp.float32)
        wide[pl.ds(piece, columns, stride=pieces), :] = block
    rows = columns * pieces
    out_ref[:rows, :] = wide[...].astype(jnp.bfloat16)
    bottom = jnp.concatenate([bottom_ref[...], jnp.zeros((1, LANES - columns), jnp.int32)], axis=1)
    row = lax.broadcasted_iota(jnp.int32, (EXTRA_ROWS, LANES), 0)
    high = lax.shift_right_logical(bottom, 8)
    extra = jnp.where(row == 0, high, jnp.where(row == 1, bottom & (CODE_BASE - 1), 0))
    out_ref[rows:, :] = extra.astype(jnp.float32).astype(jnp.bfloat16)


def spread(prop_ref, out_ref, sems):
    loads = [
        pltpu.make_async_copy(
            prop_ref.at[:, piece * LANES : (piece + 1) * LANES], out_ref.at[piece], sems.at[piece]
        )
        for piece in range(out_ref.shape[0])
    ]
    for load in loads:
        load.start()
    for load in loads:
        load.wait()


def propagate(
    track_smem, wavenumber_smem, loss_smem, tracks_ref, starter_ref, prop, own_ref, direct_ref, passed_ref,
    grid_ref, sin_table, cos_table,
    field_a, field_b, sin_a, cos_a, sin_b, cos_b, powers,
):
    pieces, double_depth, _ = prop.shape
    depth_cells = double_depth // 2
    steps, bearings = track_smem.shape
    column_total = grid_ref.shape[0]
    block_rows = own_ref.shape[0]
    cell_rows = block_rows - EXTRA_ROWS
    columns_here = cell_rows // pieces
    rounds = direct_ref.shape[0] // block_rows
    stride = pieces + 1
    per_turn = wavenumber_smem[0] * jnp.float32(QUARTER_TURN)
    decay = jnp.exp(jnp.full((pieces, LANES), -loss_smem[0], jnp.float32))
    me = lax.axis_index("bearing")
    core = lax.axis_index("freq") % 2
    owners = 2 * rounds

    def place_of(turn, unit):
        offset = owners - 1 - 2 * turn - unit
        return jnp.where(offset == 0, owners, me ^ offset)

    depth_index = lax.broadcasted_iota(jnp.int32, (pieces, LANES), 0) * LANES + lax.broadcasted_iota(
        jnp.int32, (pieces, LANES), 1
    )
    depth_index = depth_index.astype(jnp.float32)

    def tabulate(ref, place, start):
        base = place * cell_rows
        codes = ref[pl.ds(start + cell_rows, EXTRA_ROWS), :].astype(jnp.float32)
        bottoms = codes[0:1] * jnp.float32(CODE_BASE) + codes[1:2]
        bottoms = jnp.broadcast_to(bottoms, (pieces, LANES))
        for pair in range(columns_here // 2):
            both = ref[pl.ds(pl.multiple_of(start + pair * 2 * pieces, 2 * pieces), 2 * pieces), :]
            both = both.astype(jnp.float32) * per_turn
            for column in (2 * pair, 2 * pair + 1):
                inner = (column - 2 * pair) * pieces
                sine, cosine, sine_minus, cosine_minus = sine_and_cosine(both[inner : inner + pieces])
                bottom = jnp.broadcast_to(bottoms[:, column : column + 1], (pieces, LANES))
                damping = jnp.where(depth_index >= bottom, decay, jnp.float32(1.0))
                rows = pl.ds(pl.multiple_of(base + column * pieces, pieces), pieces)
                sin_table[rows, :] = sine * jnp.where(sine_minus, -damping, damping)
                cos_table[rows, :] = cosine * jnp.where(cosine_minus, -damping, damping)

    tabulate(own_ref, me, 0)
    for index, ref in enumerate((direct_ref, passed_ref)):

        def one(turn, carry, ref=ref, index=index):
            tabulate(ref, place_of(turn, core ^ index), turn * block_rows)
            return carry

        lax.fori_loop(0, rounds, one, 0)

    def put(field, cells, real, imaginary):
        beyond = slice(depth_cells + cells.start, depth_cells + cells.stop)
        field[:bearings, cells] = real
        field[:bearings, beyond] = -imaginary
        field[bearings:, cells] = imaginary
        field[bearings:, beyond] = real

    put(field_a, slice(0, depth_cells), starter_ref[:bearings, :], starter_ref[bearings:, :])

    def prepare(step, sin_ref, cos_ref, which):
        for bearing in which:
            column = track_smem[step, bearing]
            rows = pl.ds(pl.multiple_of(column * pieces, pieces), pieces)
            sin_ref[bearing * stride : bearing * stride + pieces, :] = sin_table[rows, :]
            cos_ref[bearing * stride : bearing * stride + pieces, :] = cos_table[rows, :]

    lane = lax.broadcasted_iota(jnp.int32, (bearings, LANES), 1)

    def fold(first, second, width):
        return jnp.where(
            (lane & width) == 0,
            first + pltpu.roll(first, LANES - width, 1),
            second + pltpu.roll(second, width, 1),
        )

    tiles = depth_cells // TILE
    halves = tiles // 2
    pieces_in = 2 * TILE // LANES
    early = [tile + part * tiles for tile in range(tiles - 2) for part in range(2)]
    late = [tile + part * tiles for tile in range(tiles - 2, tiles) for part in range(2)]
    slots_of_step = halves * (len(early) + len(late))
    nothing = jnp.zeros((PAD_ROWS, TILE), jnp.bfloat16)

    def run(*accumulators):
        sums, spare = accumulators[: 2 * halves], accumulators[2 * halves :]
        count = [0]

        def multiply(field, half, tile):
            register = count[0] % 2
            count[0] += 1
            cells = slice(tile * TILE, (tile + 1) * TILE)
            for unit in range(2):
                first = (2 * half + unit) * (TILE // LANES)
                weights = jnp.concatenate([prop[first, cells, :], prop[first + 1, cells, :]], axis=1)
                pltpu.matmul_push_rhs(weights, register, unit)
            for unit in range(2):
                pltpu.matmul_acc_lhs(sums[2 * half + unit], field[:, cells], load_staged_rhs=register)
                pltpu.matmul_acc_lhs(spare[unit], nothing)

        def begin(field):
            for half in range(halves):
                for tile in early:
                    multiply(field, half, tile)

        def advance(step, field, following, sin_ref, cos_ref, next_sin, next_cos):
            work = [[] for _ in range(slots_of_step + 1)]
            share = -(-bearings // slots_of_step)
            coming = jnp.minimum(step + 1, steps - 1)
            for slot in range(slots_of_step):
                which = range(slot * share, min(bearings, (slot + 1) * share))
                work[slot].append(functools.partial(prepare, coming, next_sin, next_cos, which))
            moved = {}
            folded = {}

            def pop(half):
                for unit in range(2):
                    moved[2 * half + unit] = pltpu.matmul_pop(sums[2 * half + unit])

            def screen(piece):
                value = moved[piece * LANES // TILE]
                inner = slice(piece * LANES % TILE, piece * LANES % TILE + LANES)
                moved_re = value[:bearings, inner]
                moved_im = value[bearings:, inner]
                sine = sin_ref[pl.ds(piece, bearings, stride=stride), :]
                cosine = cos_ref[pl.ds(piece, bearings, stride=stride), :]
                screened_re = moved_re * cosine - moved_im * sine
                screened_im = moved_re * sine + moved_im * cosine
                outer = slice(piece * LANES, (piece + 1) * LANES)
                put(following, outer, screened_re.astype(jnp.bfloat16), screened_im.astype(jnp.bfloat16))
                level, value = 1, screened_re * screened_re + screened_im * screened_im
                at = piece
                while at % 2 == 1:
                    value = fold(folded.pop((level, at - 1)), value, level)
                    at //= 2
                    level *= 2
                folded[level, at] = value

            for half in range(halves):
                after = (half + 1) * len(late)
                work[after].append(functools.partial(pop, half))
                for index in range(pieces_in):
                    slot = after + 1 + index
                    if half < halves - 1:
                        slot = min(slot, after + len(late) - 1)
                    work[min(slot, slots_of_step)].append(functools.partial(screen, half * pieces_in + index))
            slot = 0
            for source, order in ((field, late), (following, early)):
                for half in range(halves):
                    for tile in order:
                        multiply(source, half, tile)
                        for item in work[slot]:
                            item()
                        slot += 1
            for item in work[slot]:
                item()
            rows = pl.ds(pl.multiple_of(step * bearings, bearings), bearings)
            powers[rows, :] = folded[pieces, 0]

        begin(field_a)
        prepare(0, sin_a, cos_a, range(bearings))

        together = 4 if steps % 4 == 0 else 2

        def some_steps(index, carry):
            for step in range(0, together, 2):
                advance(index * together + step, field_a, field_b, sin_a, cos_a, sin_b, cos_b)
                advance(index * together + step + 1, field_b, field_a, sin_b, cos_b, sin_a, cos_a)
            return carry

        lax.fori_loop(0, steps // together, some_steps, 0)
        for accumulator in accumulators:
            pltpu.matmul_pop(accumulator)

    pl.run_scoped(
        run,
        *[pltpu.ACC(unit % 2)((2 * bearings, TILE), jnp.float32) for unit in range(2 * halves)],
        *[pltpu.ACC(unit)((PAD_ROWS, TILE), jnp.float32) for unit in range(2)],
    )

    group = TILE // bearings
    lanes_of_row = lax.broadcasted_iota(jnp.int32, (1, LANES), 1)

    def ids_of(first):
        parts = []
        for start in range(first, first + group, LANES // bearings):
            row = tracks_ref[start : start + 1, :]
            total = jnp.concatenate([row, jnp.zeros((1, LANES - bearings), jnp.int32)], axis=1)
            for index in range(1, LANES // bearings):
                row = tracks_ref[start + index : start + index + 1, :]
                row = jnp.concatenate([row, jnp.zeros((1, LANES - bearings), jnp.int32)], axis=1)
                total = total + pltpu.roll(row, index * bearings, 1)
            parts.append(total)
        return jnp.concatenate(parts, axis=1)

    half_columns = column_total // 2

    def scatter(*sums):
        for index, start in enumerate(range(0, steps, group)):
            ids = ids_of(start)
            value = powers[start * bearings : (start + group) * bearings, :]
            high = value.astype(jnp.bfloat16)
            low = (value - high.astype(jnp.float32)).astype(jnp.bfloat16)
            both = jnp.concatenate([high, low], axis=1)
            for unit in range(2):
                pltpu.matmul_push_rhs(both, index % 2, unit)
            for unit in range(2):
                column = lax.broadcasted_iota(jnp.int32, (half_columns, TILE), 0) + unit * half_columns
                chosen = (column == ids).astype(jnp.bfloat16)
                pltpu.matmul_acc_lhs(sums[unit], chosen, load_staged_rhs=index % 2)
        for unit in range(2):
            total = pltpu.matmul_pop(sums[unit])
            grid_ref[unit * half_columns : (unit + 1) * half_columns, :] = total[:, :LANES] + total[:, LANES:]

    pl.run_scoped(scatter, *[pltpu.ACC(unit)((half_columns, TILE), jnp.float32) for unit in range(2)])


def finish(scale, parts_ref, out_ref):
    total = jnp.sum(parts_ref[...].astype(jnp.float32), axis=0) * jnp.float32(scale)
    row = lax.broadcasted_iota(jnp.int32, (LANES, LANES), 0)
    column = lax.broadcasted_iota(jnp.int32, (LANES, LANES), 1)
    groups = LANES // BAND_CELLS
    place = (row % BAND_CELLS) * groups + row // BAND_CELLS
    order = (place == column).astype(jnp.bfloat16)
    rows = total.shape[0]
    parts = []
    for _ in range(3):
        part = total.astype(jnp.bfloat16)
        total = total - part.astype(jnp.float32)
        parts.append(part.astype(jnp.float32))
    parts = jnp.concatenate(parts, axis=0).astype(jnp.bfloat16)
    placed = jnp.dot(parts, order, preferred_element_type=jnp.float32)
    out_ref[...] = placed[:rows] + (placed[rows : 2 * rows] + placed[2 * rows :])


def on_device(starter, propagator, wavenumber, sediment_loss, env_speed, bottom, track_column):
    bearings_here, steps = track_column.shape
    columns_here, depth_cells = env_speed.shape
    bands = depth_cells // BAND_CELLS
    owners = lax.axis_size("bearing")
    freqs = lax.axis_size("freq")
    devices = owners * freqs
    column_total = columns_here * owners
    pieces = depth_cells // LANES
    smem = pl.BlockSpec(memory_space=pltpu.SMEM)
    vmem = pl.BlockSpec(memory_space=pltpu.VMEM)

    own = pl.pallas_call(
        pack,
        out_shape=jax.ShapeDtypeStruct((columns_here * pieces + EXTRA_ROWS, LANES), jnp.bfloat16),
        in_specs=[vmem] * 2,
        out_specs=vmem,
        scratch_shapes=[pltpu.VMEM((columns_here * pieces, LANES), jnp.float32)],
        name="pack",
    )(env_speed, bottom.reshape(1, -1))

    turns = [(offset, offset - 1) for offset in range(owners - 1, 0, -2)]
    received = []
    for turn in turns:
        pairs = [
            (bearing * freqs + freq, (bearing ^ turn[freq % 2]) * freqs + freq)
            for bearing in range(owners)
            for freq in range(freqs)
            if turn[freq % 2]
        ]
        received.append(lax.ppermute(own, ("bearing", "freq"), pairs))
    spread_out = pl.pallas_call(
        spread,
        out_shape=jax.ShapeDtypeStruct((pieces, 2 * depth_cells, LANES), jnp.bfloat16),
        in_specs=[pl.BlockSpec(memory_space=pl.ANY)],
        out_specs=vmem,
        scratch_shapes=[pltpu.SemaphoreType.DMA((pieces,))],
        compiler_params=pltpu.CompilerParams(vmem_limit_bytes=SPREAD_LIMIT),
        cost_estimate=pl.CostEstimate(flops=0, bytes_accessed=2 * propagator.size * 2, transcendentals=0),
        name="spread",
    )(propagator[0].reshape(2 * depth_cells, depth_cells))
    direct = jnp.concatenate(received, axis=0)
    direct, spread_out = lax.optimization_barrier((direct, spread_out))
    passed = lax.ppermute(direct, "freq", [(freq, freq ^ 1) for freq in range(freqs)])

    tracks = track_column.T
    grid = pl.pallas_call(
        propagate,
        out_shape=jax.ShapeDtypeStruct((column_total, bands), jnp.float32),
        in_specs=[smem] * 3 + [vmem] * 6,
        out_specs=vmem,
        scratch_shapes=[
            pltpu.VMEM(((owners + 1) * columns_here * pieces, LANES), jnp.float32),
            pltpu.VMEM(((owners + 1) * columns_here * pieces, LANES), jnp.float32),
        ]
        + [pltpu.VMEM((2 * bearings_here, 2 * depth_cells), jnp.bfloat16)] * 2
        + [pltpu.VMEM((bearings_here * (pieces + 1), LANES), jnp.float32)] * 4
        + [pltpu.VMEM((steps * bearings_here, bands), jnp.float32)],
        compiler_params=pltpu.CompilerParams(vmem_limit_bytes=VMEM_LIMIT),
        name="propagate",
    )(
        tracks, wavenumber, sediment_loss, tracks, starter[0].reshape(2 * bearings_here, depth_cells),
        spread_out, own, direct, passed,
    )
    parts = lax.all_to_all(
        grid.reshape(devices, column_total // devices, bands), ("bearing", "freq"), 0, 0
    )
    scale = column_total / (bearings_here * owners * steps * freqs)
    return pl.pallas_call(
        functools.partial(finish, scale),
        out_shape=jax.ShapeDtypeStruct((column_total // devices, bands), jnp.float32),
        in_specs=[vmem],
        out_specs=vmem,
        name="finish",
    )(parts)


def solution(mesh):
    in_specs = (
        P("freq", None, "bearing", None),
        P("freq", None, None, None),
        P("freq"),
        P("freq"),
        P("bearing", None),
        P("bearing"),
        P("bearing", None),
    )
    out_specs = P(("bearing", "freq"), None)
    mapped = jax.shard_map(
        on_device, mesh=mesh, in_specs=in_specs, out_specs=out_specs, check_vma=False
    )

    def program(*arrays):
        with jax.sharding.use_abstract_mesh(mesh.abstract_mesh):
            return mapped(*arrays)

    return program
```

```python
import functools

import jax
import jax.numpy as jnp
from jax import lax
from jax.experimental import pallas as pl
from jax.experimental.pallas import tpu as pltpu
from jax.sharding import PartitionSpec as P

BAND_CELLS = 8
LANES = 128
TILE = 256
PAD_ROWS = 64
EXTRA_ROWS = 16
CODE_BASE = 256
HALF_TURN = 0.3183098861837907
SIN_TERMS = (3.141592640130706, -5.167710083507879, 2.550077523214355, -0.598291285618806, 0.07765766030210168)
COS_TERMS = (0.9999999532476083, -4.9347928306196405, 4.058411352862505, -1.3318765680803568, 0.2196896110969353)
TOGETHER = (8, 4, 2)
VMEM_LIMIT = 24 * 1024 * 1024
SPREAD_LIMIT = 24 * 1024 * 1024


def polynomial(terms, square):
    total = jnp.float32(terms[-1])
    for term in terms[-2::-1]:
        total = total * square + jnp.float32(term)
    return total


def sine_and_cosine(turns):
    nearest = jnp.round(turns)
    rest = turns - nearest
    square = rest * rest
    sine = polynomial(SIN_TERMS, square) * rest
    cosine = polynomial(COS_TERMS, square)
    return sine, cosine, (nearest.astype(jnp.int32) & 1) != 0


def parity(number):
    number = number ^ (number >> 4)
    number = number ^ (number >> 2)
    return (number ^ (number >> 1)) & 1


def pack(env_ref, bottom_ref, out_ref, wide):
    columns, depth_cells = env_ref.shape
    pieces = depth_cells // LANES
    for piece in range(pieces):
        block = env_ref[:, piece * LANES : (piece + 1) * LANES].astype(jnp.float32)
        wide[pl.ds(piece, columns, stride=pieces), :] = block
    rows = columns * pieces
    out_ref[:rows, :] = wide[...].astype(jnp.bfloat16)
    bottom = jnp.concatenate([bottom_ref[...], jnp.zeros((1, LANES - columns), jnp.int32)], axis=1)
    row = lax.broadcasted_iota(jnp.int32, (EXTRA_ROWS, LANES), 0)
    high = lax.shift_right_logical(bottom, 8)
    extra = jnp.where(row == 0, high, jnp.where(row == 1, bottom & (CODE_BASE - 1), 0))
    out_ref[rows:, :] = extra.astype(jnp.float32).astype(jnp.bfloat16)


def spread(prop_ref, out_ref, sems):
    loads = [
        pltpu.make_async_copy(
            prop_ref.at[:, piece * LANES : (piece + 1) * LANES], out_ref.at[piece], sems.at[piece]
        )
        for piece in range(out_ref.shape[0])
    ]
    for load in loads:
        load.start()
    for load in loads:
        load.wait()


def propagate(
    track_smem, wavenumber_smem, loss_smem, tracks_ref, starter_ref, prop, own_ref, direct_ref, passed_ref,
    grid_ref, sin_table, cos_table, bottom_rows,
    field_a, field_b, sin_a, cos_a, sin_b, cos_b, powers,
):
    pieces, double_depth, _ = prop.shape
    depth_cells = double_depth // 2
    steps, bearings = track_smem.shape
    column_total = grid_ref.shape[0]
    block_rows = own_ref.shape[0]
    cell_rows = block_rows - EXTRA_ROWS
    columns_here = cell_rows // pieces
    rounds = direct_ref.shape[0] // block_rows
    stride = pieces + 1
    per_turn = wavenumber_smem[0] * jnp.float32(HALF_TURN)
    decay = jnp.exp(jnp.full((pieces, LANES), -loss_smem[0], jnp.float32))
    me = lax.axis_index("bearing")
    core = lax.axis_index("freq") % 2

    def place_of(turn, unit):
        return me ^ (2 * turn + (parity(turn) ^ 1 ^ unit))

    depth_index = lax.broadcasted_iota(jnp.int32, (pieces, LANES), 0) * LANES + lax.broadcasted_iota(
        jnp.int32, (pieces, LANES), 1
    )
    depth_index = depth_index.astype(jnp.float32)

    def tabulate(ref, place, start):
        base = place * cell_rows
        codes = ref[pl.ds(start + cell_rows, EXTRA_ROWS), :].astype(jnp.float32)
        bottoms = codes[0:1] * jnp.float32(CODE_BASE) + codes[1:2]
        own_lane = lax.broadcasted_iota(jnp.int32, (columns_here, LANES), 0) == lax.broadcasted_iota(
            jnp.int32, (columns_here, LANES), 1
        )
        bottoms = jnp.sum(jnp.where(own_lane, bottoms, jnp.float32(0)), axis=1, keepdims=True)
        bottom_rows[...] = jnp.broadcast_to(bottoms, (columns_here, LANES))
        for pair in range(columns_here // 2):
            both = ref[pl.ds(pl.multiple_of(start + pair * 2 * pieces, 2 * pieces), 2 * pieces), :]
            both = both.astype(jnp.float32) * per_turn
            for column in (2 * pair, 2 * pair + 1):
                inner = (column - 2 * pair) * pieces
                sine, cosine, minus = sine_and_cosine(both[inner : inner + pieces])
                bottom = bottom_rows[column : column + 1, :]
                damping = jnp.where(depth_index >= bottom, decay, jnp.float32(1.0))
                rows = pl.ds(pl.multiple_of(base + column * pieces, pieces), pieces)
                damping = jnp.where(minus, -damping, damping)
                sin_table[rows, :] = sine * damping
                cos_table[rows, :] = cosine * damping

    for index, ref in enumerate((direct_ref, passed_ref)):

        def one(turn, carry, ref=ref, index=index):
            place = place_of(turn, core ^ index)

            @pl.when(place != me)
            def _():
                tabulate(ref, place, turn * block_rows)

            return carry

        lax.fori_loop(0, rounds, one, 0)

    def put(field, cells, real, imaginary):
        beyond = slice(depth_cells + cells.start, depth_cells + cells.stop)
        field[:bearings, cells] = real
        field[:bearings, beyond] = -imaginary
        field[bearings:, cells] = imaginary
        field[bearings:, beyond] = real

    put(field_a, slice(0, depth_cells), starter_ref[:bearings, :], starter_ref[bearings:, :])

    def prepare(step, sin_ref, cos_ref, which):
        for bearing in which:
            column = track_smem[step, bearing]
            rows = pl.ds(pl.multiple_of(column * pieces, pieces), pieces)
            sin_ref[bearing * stride : bearing * stride + pieces, :] = sin_table[rows, :]
            cos_ref[bearing * stride : bearing * stride + pieces, :] = cos_table[rows, :]

    lane = lax.broadcasted_iota(jnp.int32, (bearings, LANES), 1)

    def fold(first, second, width):
        return jnp.where(
            (lane & width) == 0,
            first + pltpu.roll(first, LANES - width, 1),
            second + pltpu.roll(second, width, 1),
        )

    tiles = depth_cells // TILE
    halves = tiles // 2
    pieces_in = 2 * TILE // LANES
    early = [tile + part * tiles for tile in range(tiles - 2) for part in range(2)]
    late = [tile + part * tiles for tile in range(tiles - 2, tiles) for part in range(2)]
    slots_of_step = halves * (len(early) + len(late))
    nothing = jnp.zeros((PAD_ROWS, TILE), jnp.bfloat16)

    def run(*accumulators):
        sums, spare = accumulators[: 2 * halves], accumulators[2 * halves :]
        count = [0]

        def multiply(field, half, tile):
            register = count[0] % 2
            count[0] += 1
            cells = slice(tile * TILE, (tile + 1) * TILE)
            for unit in range(2):
                first = (2 * half + unit) * (TILE // LANES)
                weights = jnp.concatenate([prop[first, cells, :], prop[first + 1, cells, :]], axis=1)
                pltpu.matmul_push_rhs(weights, register, unit)
            for unit in range(2):
                pltpu.matmul_acc_lhs(sums[2 * half + unit], field[:, cells], load_staged_rhs=register)
                pltpu.matmul_acc_lhs(spare[unit], nothing)

        def begin(field):
            for half in range(halves):
                for tile in early:
                    multiply(field, half, tile)

        def advance(step, field, following, sin_ref, cos_ref, next_sin, next_cos, last=False):
            work = [[] for _ in range(slots_of_step + 1)]
            share = -(-bearings // slots_of_step)
            for slot in range(0 if last else slots_of_step):
                which = range(slot * share, min(bearings, (slot + 1) * share))
                work[slot].append(functools.partial(prepare, step + 1, next_sin, next_cos, which))
            moved = {}
            folded = {}

            def pop(half):
                for unit in range(2):
                    moved[2 * half + unit] = pltpu.matmul_pop(sums[2 * half + unit])

            def screen(piece):
                value = moved[piece * LANES // TILE]
                inner = slice(piece * LANES % TILE, piece * LANES % TILE + LANES)
                moved_re = value[:bearings, inner]
                moved_im = value[bearings:, inner]
                sine = sin_ref[pl.ds(piece, bearings, stride=stride), :]
                cosine = cos_ref[pl.ds(piece, bearings, stride=stride), :]
                screened_re = moved_re * cosine - moved_im * sine
                screened_im = moved_re * sine + moved_im * cosine
                outer = slice(piece * LANES, (piece + 1) * LANES)
                put(following, outer, screened_re.astype(jnp.bfloat16), screened_im.astype(jnp.bfloat16))
                level, value = 1, screened_re * screened_re + screened_im * screened_im
                at = piece
                while at % 2 == 1:
                    value = fold(folded.pop((level, at - 1)), value, level)
                    at //= 2
                    level *= 2
                folded[level, at] = value

            for half in range(halves):
                after = (half + 1) * len(late)
                work[after].append(functools.partial(pop, half))
                for index in range(pieces_in):
                    slot = after + 1 + index
                    if half < halves - 1:
                        slot = min(slot, after + len(late) - 1)
                    work[min(slot, slots_of_step)].append(functools.partial(screen, half * pieces_in + index))
            slot = 0
            for source, order in ((field, late), (following, early)):
                for half in range(halves):
                    for tile in order:
                        if source is field or not last:
                            multiply(source, half, tile)
                        for item in work[slot]:
                            item()
                        slot += 1
            for item in work[slot]:
                item()
            rows = pl.ds(pl.multiple_of(step * bearings, bearings), bearings)
            powers[rows, :] = folded[pieces, 0]

        begin(field_a)
        tabulate(own_ref, me, 0)
        prepare(0, sin_a, cos_a, range(bearings))

        together = next(number for number in TOGETHER if steps % number == 0)

        def some_steps(index, carry, last=False):
            for step in range(0, together, 2):
                advance(index * together + step, field_a, field_b, sin_a, cos_a, sin_b, cos_b)
                ends = last and step + 2 == together
                advance(index * together + step + 1, field_b, field_a, sin_b, cos_b, sin_a, cos_a, ends)
            return carry

        lax.fori_loop(0, steps // together - 1, some_steps, 0)
        some_steps(steps // together - 1, 0, True)
        for accumulator in spare:
            pltpu.matmul_pop(accumulator)

    pl.run_scoped(
        run,
        *[pltpu.ACC(unit % 2)((2 * bearings, TILE), jnp.float32) for unit in range(2 * halves)],
        *[pltpu.ACC(unit)((PAD_ROWS, TILE), jnp.float32) for unit in range(2)],
    )

    group = TILE // bearings
    lanes_of_row = lax.broadcasted_iota(jnp.int32, (1, LANES), 1)

    def ids_of(first):
        parts = []
        for start in range(first, first + group, LANES // bearings):
            row = tracks_ref[start : start + 1, :]
            total = jnp.concatenate([row, jnp.zeros((1, LANES - bearings), jnp.int32)], axis=1)
            for index in range(1, LANES // bearings):
                row = tracks_ref[start + index : start + index + 1, :]
                row = jnp.concatenate([row, jnp.zeros((1, LANES - bearings), jnp.int32)], axis=1)
                total = total + pltpu.roll(row, index * bearings, 1)
            parts.append(total)
        return jnp.concatenate(parts, axis=1)

    half_columns = column_total // 2

    def scatter(*sums):
        for index, start in enumerate(range(0, steps, group)):
            ids = ids_of(start)
            value = powers[start * bearings : (start + group) * bearings, :]
            high = value.astype(jnp.bfloat16)
            low = (value - high.astype(jnp.float32)).astype(jnp.bfloat16)
            both = jnp.concatenate([high, low], axis=1)
            for unit in range(2):
                pltpu.matmul_push_rhs(both, index % 2, unit)
            for unit in range(2):
                column = lax.broadcasted_iota(jnp.int32, (half_columns, TILE), 0) + unit * half_columns
                chosen = (column == ids).astype(jnp.bfloat16)
                pltpu.matmul_acc_lhs(sums[unit], chosen, load_staged_rhs=index % 2)
        for unit in range(2):
            total = pltpu.matmul_pop(sums[unit])
            grid_ref[unit * half_columns : (unit + 1) * half_columns, :] = total[:, :LANES] + total[:, LANES:]

    pl.run_scoped(scatter, *[pltpu.ACC(unit)((half_columns, TILE), jnp.float32) for unit in range(2)])


def finish(scale, parts_ref, out_ref):
    total = jnp.sum(parts_ref[...].astype(jnp.float32), axis=0) * jnp.float32(scale)
    row = lax.broadcasted_iota(jnp.int32, (LANES, LANES), 0)
    column = lax.broadcasted_iota(jnp.int32, (LANES, LANES), 1)
    groups = LANES // BAND_CELLS
    place = (row % BAND_CELLS) * groups + row // BAND_CELLS
    order = (place == column).astype(jnp.bfloat16)
    rows = total.shape[0]
    parts = []
    for _ in range(3):
        part = total.astype(jnp.bfloat16)
        total = total - part.astype(jnp.float32)
        parts.append(part.astype(jnp.float32))
    parts = jnp.concatenate(parts, axis=0).astype(jnp.bfloat16)
    placed = jnp.dot(parts, order, preferred_element_type=jnp.float32)
    out_ref[...] = placed[:rows] + (placed[rows : 2 * rows] + placed[2 * rows :])


def on_device(starter, propagator, wavenumber, sediment_loss, env_speed, bottom, track_column):
    bearings_here, steps = track_column.shape
    columns_here, depth_cells = env_speed.shape
    bands = depth_cells // BAND_CELLS
    owners = lax.axis_size("bearing")
    freqs = lax.axis_size("freq")
    devices = owners * freqs
    column_total = columns_here * owners
    pieces = depth_cells // LANES
    smem = pl.BlockSpec(memory_space=pltpu.SMEM)
    vmem = pl.BlockSpec(memory_space=pltpu.VMEM)

    own = pl.pallas_call(
        pack,
        out_shape=jax.ShapeDtypeStruct((columns_here * pieces + EXTRA_ROWS, LANES), jnp.bfloat16),
        in_specs=[vmem] * 2,
        out_specs=vmem,
        scratch_shapes=[pltpu.VMEM((columns_here * pieces, LANES), jnp.float32)],
        name="pack",
    )(env_speed, bottom.reshape(1, -1))

    turns = [(2 * turn + 1 - parity(turn), 2 * turn + parity(turn)) for turn in range(owners // 2)]
    received = []
    for turn in turns:
        pairs = [
            (bearing * freqs + freq, (bearing ^ turn[freq % 2]) * freqs + freq)
            for bearing in range(owners)
            for freq in range(freqs)
            if turn[freq % 2]
        ]
        received.append(lax.ppermute(own, ("bearing", "freq"), pairs))
    spread_out = pl.pallas_call(
        spread,
        out_shape=jax.ShapeDtypeStruct((pieces, 2 * depth_cells, LANES), jnp.bfloat16),
        in_specs=[pl.BlockSpec(memory_space=pl.ANY)],
        out_specs=vmem,
        scratch_shapes=[pltpu.SemaphoreType.DMA((pieces,))],
        compiler_params=pltpu.CompilerParams(vmem_limit_bytes=SPREAD_LIMIT),
        cost_estimate=pl.CostEstimate(flops=0, bytes_accessed=2 * propagator.size * 2, transcendentals=0),
        name="spread",
    )(propagator[0].reshape(2 * depth_cells, depth_cells))
    direct = jnp.concatenate(received, axis=0)
    direct, spread_out = lax.optimization_barrier((direct, spread_out))
    passed = lax.ppermute(direct, "freq", [(freq, freq ^ 1) for freq in range(freqs)])

    tracks = track_column.T
    grid = pl.pallas_call(
        propagate,
        out_shape=jax.ShapeDtypeStruct((column_total, bands), jnp.float32),
        in_specs=[smem] * 3 + [vmem] * 6,
        out_specs=vmem,
        scratch_shapes=[
            pltpu.VMEM((owners * columns_here * pieces, LANES), jnp.float32),
            pltpu.VMEM((owners * columns_here * pieces, LANES), jnp.float32),
            pltpu.VMEM((columns_here, LANES), jnp.float32),
        ]
        + [pltpu.VMEM((2 * bearings_here, 2 * depth_cells), jnp.bfloat16)] * 2
        + [pltpu.VMEM((bearings_here * (pieces + 1), LANES), jnp.float32)] * 4
        + [pltpu.VMEM((steps * bearings_here, bands), jnp.float32)],
        compiler_params=pltpu.CompilerParams(vmem_limit_bytes=VMEM_LIMIT),
        name="propagate",
    )(
        tracks, wavenumber, sediment_loss, tracks, starter[0].reshape(2 * bearings_here, depth_cells),
        spread_out, own, direct, passed,
    )
    parts = lax.all_to_all(
        grid.reshape(devices, column_total // devices, bands), ("bearing", "freq"), 0, 0
    )
    scale = column_total / (bearings_here * owners * steps * freqs)
    return pl.pallas_call(
        functools.partial(finish, scale),
        out_shape=jax.ShapeDtypeStruct((column_total // devices, bands), jnp.float32),
        in_specs=[vmem],
        out_specs=vmem,
        name="finish",
    )(parts)


def solution(mesh):
    in_specs = (
        P("freq", None, "bearing", None),
        P("freq", None, None, None),
        P("freq"),
        P("freq"),
        P("bearing", None),
        P("bearing"),
        P("bearing", None),
    )
    out_specs = P(("bearing", "freq"), None)
    mapped = jax.shard_map(
        on_device, mesh=mesh, in_specs=in_specs, out_specs=out_specs, check_vma=False
    )

    def program(*arrays):
        with jax.sharding.use_abstract_mesh(mesh.abstract_mesh):
            return mapped(*arrays)

    return program
```

```python
import functools

import jax
import jax.numpy as jnp
from jax import lax
from jax.experimental import pallas as pl
from jax.experimental.pallas import tpu as pltpu
from jax.sharding import PartitionSpec as P

BAND_CELLS = 8
LANES = 128
TILE = 256
PAD_ROWS = 64
EXTRA_ROWS = 16
CODE_BASE = 256
HALF_TURN = 0.3183098861837907
SIN_TERMS = (3.141592640130706, -5.167710083507879, 2.550077523214355, -0.598291285618806, 0.07765766030210168)
COS_TERMS = (0.9999999532476083, -4.9347928306196405, 4.058411352862505, -1.3318765680803568, 0.2196896110969353)
TOGETHER = (8, 4, 2)
VMEM_LIMIT = 24 * 1024 * 1024
SPREAD_LIMIT = 24 * 1024 * 1024


def polynomial(terms, square):
    total = jnp.float32(terms[-1])
    for term in terms[-2::-1]:
        total = total * square + jnp.float32(term)
    return total


def sine_and_cosine(turns):
    nearest = jnp.round(turns)
    rest = turns - nearest
    square = rest * rest
    sine = polynomial(SIN_TERMS, square) * rest
    cosine = polynomial(COS_TERMS, square)
    return sine, cosine, (nearest.astype(jnp.int32) & 1) != 0


def parity(number):
    number = number ^ (number >> 4)
    number = number ^ (number >> 2)
    return (number ^ (number >> 1)) & 1


def pack(env_ref, bottom_ref, out_ref, wide):
    columns, depth_cells = env_ref.shape
    pieces = depth_cells // LANES
    for piece in range(pieces):
        block = env_ref[:, piece * LANES : (piece + 1) * LANES].astype(jnp.float32)
        wide[pl.ds(piece, columns, stride=pieces), :] = block
    rows = columns * pieces
    out_ref[:rows, :] = wide[...].astype(jnp.bfloat16)
    bottom = jnp.concatenate([bottom_ref[...], jnp.zeros((1, LANES - columns), jnp.int32)], axis=1)
    row = lax.broadcasted_iota(jnp.int32, (EXTRA_ROWS, LANES), 0)
    high = lax.shift_right_logical(bottom, 8)
    extra = jnp.where(row == 0, high, jnp.where(row == 1, bottom & (CODE_BASE - 1), 0))
    out_ref[rows:, :] = extra.astype(jnp.float32).astype(jnp.bfloat16)


def spread(prop_ref, out_ref, sems):
    loads = [
        pltpu.make_async_copy(
            prop_ref.at[:, piece * LANES : (piece + 1) * LANES], out_ref.at[piece], sems.at[piece]
        )
        for piece in range(out_ref.shape[0])
    ]
    for load in loads:
        load.start()
    for load in loads:
        load.wait()


def propagate(
    turns,
    track_smem, wavenumber_smem, loss_smem, tracks_ref, starter_ref, prop, own_ref, direct_ref, passed_ref,
    grid_ref, sin_table, cos_table, bottom_rows,
    field_a, field_b, sin_a, cos_a, sin_b, cos_b, powers,
):
    pieces, double_depth, _ = prop.shape
    depth_cells = double_depth // 2
    steps, bearings = track_smem.shape
    column_total = grid_ref.shape[0]
    block_rows = own_ref.shape[0]
    cell_rows = block_rows - EXTRA_ROWS
    columns_here = cell_rows // pieces
    rounds = direct_ref.shape[0] // block_rows
    stride = pieces + 1
    per_turn = wavenumber_smem[0] * jnp.float32(HALF_TURN)
    decay = jnp.exp(jnp.full((pieces, LANES), -loss_smem[0], jnp.float32))
    me = lax.axis_index("bearing")
    core = lax.axis_index("freq") % 2

    def place_of(turn, unit):
        offset = jnp.int32(0)
        for index, pair in enumerate(turns):
            offset = jnp.where(turn == index, jnp.where(unit == 0, pair[0], pair[1]), offset)
        return me ^ offset

    depth_index = lax.broadcasted_iota(jnp.int32, (pieces, LANES), 0) * LANES + lax.broadcasted_iota(
        jnp.int32, (pieces, LANES), 1
    )
    depth_index = depth_index.astype(jnp.float32)

    def tabulate(ref, place, start):
        base = place * cell_rows
        codes = ref[pl.ds(start + cell_rows, EXTRA_ROWS), :].astype(jnp.float32)
        bottoms = codes[0:1] * jnp.float32(CODE_BASE) + codes[1:2]
        own_lane = lax.broadcasted_iota(jnp.int32, (columns_here, LANES), 0) == lax.broadcasted_iota(
            jnp.int32, (columns_here, LANES), 1
        )
        bottoms = jnp.sum(jnp.where(own_lane, bottoms, jnp.float32(0)), axis=1, keepdims=True)
        bottom_rows[...] = jnp.broadcast_to(bottoms, (columns_here, LANES))
        for pair in range(columns_here // 2):
            both = ref[pl.ds(pl.multiple_of(start + pair * 2 * pieces, 2 * pieces), 2 * pieces), :]
            both = both.astype(jnp.float32) * per_turn
            for column in (2 * pair, 2 * pair + 1):
                inner = (column - 2 * pair) * pieces
                sine, cosine, minus = sine_and_cosine(both[inner : inner + pieces])
                bottom = bottom_rows[column : column + 1, :]
                damping = jnp.where(depth_index >= bottom, decay, jnp.float32(1.0))
                rows = pl.ds(pl.multiple_of(base + column * pieces, pieces), pieces)
                damping = jnp.where(minus, -damping, damping)
                sin_table[rows, :] = sine * damping
                cos_table[rows, :] = cosine * damping

    for index, ref in enumerate((direct_ref, passed_ref)):

        def one(turn, carry, ref=ref, index=index):
            place = place_of(turn, core ^ index)

            @pl.when(place != me)
            def _():
                tabulate(ref, place, turn * block_rows)

            return carry

        lax.fori_loop(0, rounds, one, 0)

    def put(field, cells, real, imaginary):
        beyond = slice(depth_cells + cells.start, depth_cells + cells.stop)
        field[:bearings, cells] = real
        field[:bearings, beyond] = -imaginary
        field[bearings:, cells] = imaginary
        field[bearings:, beyond] = real

    put(field_a, slice(0, depth_cells), starter_ref[:bearings, :], starter_ref[bearings:, :])

    def prepare(step, sin_ref, cos_ref, which):
        for bearing in which:
            column = track_smem[step, bearing]
            rows = pl.ds(pl.multiple_of(column * pieces, pieces), pieces)
            sin_ref[bearing * stride : bearing * stride + pieces, :] = sin_table[rows, :]
            cos_ref[bearing * stride : bearing * stride + pieces, :] = cos_table[rows, :]

    lane = lax.broadcasted_iota(jnp.int32, (bearings, LANES), 1)

    def fold(first, second, width):
        return jnp.where(
            (lane & width) == 0,
            first + pltpu.roll(first, LANES - width, 1),
            second + pltpu.roll(second, width, 1),
        )

    tiles = depth_cells // TILE
    halves = tiles // 2
    pieces_in = 2 * TILE // LANES
    early = [tile + part * tiles for tile in range(tiles - 2) for part in range(2)]
    late = [tile + part * tiles for tile in range(tiles - 2, tiles) for part in range(2)]
    slots_of_step = halves * (len(early) + len(late))
    nothing = jnp.zeros((PAD_ROWS, TILE), jnp.bfloat16)

    def run(*accumulators):
        sums, spare = accumulators[: 2 * halves], accumulators[2 * halves :]
        count = [0]

        def multiply(field, half, tile):
            register = count[0] % 2
            count[0] += 1
            cells = slice(tile * TILE, (tile + 1) * TILE)
            for unit in range(2):
                first = (2 * half + unit) * (TILE // LANES)
                weights = jnp.concatenate([prop[first, cells, :], prop[first + 1, cells, :]], axis=1)
                pltpu.matmul_push_rhs(weights, register, unit)
            for unit in range(2):
                pltpu.matmul_acc_lhs(sums[2 * half + unit], field[:, cells], load_staged_rhs=register)
                pltpu.matmul_acc_lhs(spare[unit], nothing)

        def begin(field):
            for half in range(halves):
                for tile in early:
                    multiply(field, half, tile)

        def advance(step, field, following, sin_ref, cos_ref, next_sin, next_cos, last=False):
            work = [[] for _ in range(slots_of_step + 1)]
            share = -(-bearings // slots_of_step)
            for slot in range(0 if last else slots_of_step):
                which = range(slot * share, min(bearings, (slot + 1) * share))
                work[slot].append(functools.partial(prepare, step + 1, next_sin, next_cos, which))
            moved = {}
            folded = {}

            def pop(half):
                for unit in range(2):
                    moved[2 * half + unit] = pltpu.matmul_pop(sums[2 * half + unit])

            def screen(piece):
                value = moved[piece * LANES // TILE]
                inner = slice(piece * LANES % TILE, piece * LANES % TILE + LANES)
                moved_re = value[:bearings, inner]
                moved_im = value[bearings:, inner]
                sine = sin_ref[pl.ds(piece, bearings, stride=stride), :]
                cosine = cos_ref[pl.ds(piece, bearings, stride=stride), :]
                screened_re = moved_re * cosine - moved_im * sine
                screened_im = moved_re * sine + moved_im * cosine
                outer = slice(piece * LANES, (piece + 1) * LANES)
                put(following, outer, screened_re.astype(jnp.bfloat16), screened_im.astype(jnp.bfloat16))
                level, value = 1, screened_re * screened_re + screened_im * screened_im
                at = piece
                while at % 2 == 1:
                    value = fold(folded.pop((level, at - 1)), value, level)
                    at //= 2
                    level *= 2
                folded[level, at] = value

            for half in range(halves):
                after = (half + 1) * len(late)
                work[after].append(functools.partial(pop, half))
                for index in range(pieces_in):
                    slot = after + 1 + index
                    if half < halves - 1:
                        slot = min(slot, after + len(late) - 1)
                    work[min(slot, slots_of_step)].append(functools.partial(screen, half * pieces_in + index))
            slot = 0
            for source, order in ((field, late), (following, early)):
                for half in range(halves):
                    for tile in order:
                        if source is field or not last:
                            multiply(source, half, tile)
                        for item in work[slot]:
                            item()
                        slot += 1
            for item in work[slot]:
                item()
            rows = pl.ds(pl.multiple_of(step * bearings, bearings), bearings)
            powers[rows, :] = folded[pieces, 0]

        begin(field_a)
        tabulate(own_ref, me, 0)
        prepare(0, sin_a, cos_a, range(bearings))

        together = next(number for number in TOGETHER if steps % number == 0)

        def some_steps(index, carry, last=False):
            for step in range(0, together, 2):
                advance(index * together + step, field_a, field_b, sin_a, cos_a, sin_b, cos_b)
                ends = last and step + 2 == together
                advance(index * together + step + 1, field_b, field_a, sin_b, cos_b, sin_a, cos_a, ends)
            return carry

        lax.fori_loop(0, steps // together - 1, some_steps, 0)
        some_steps(steps // together - 1, 0, True)
        for accumulator in spare:
            pltpu.matmul_pop(accumulator)

    pl.run_scoped(
        run,
        *[pltpu.ACC(unit % 2)((2 * bearings, TILE), jnp.float32) for unit in range(2 * halves)],
        *[pltpu.ACC(unit)((PAD_ROWS, TILE), jnp.float32) for unit in range(2)],
    )

    group = TILE // bearings
    lanes_of_row = lax.broadcasted_iota(jnp.int32, (1, LANES), 1)

    def ids_of(first):
        parts = []
        for start in range(first, first + group, LANES // bearings):
            row = tracks_ref[start : start + 1, :]
            total = jnp.concatenate([row, jnp.zeros((1, LANES - bearings), jnp.int32)], axis=1)
            for index in range(1, LANES // bearings):
                row = tracks_ref[start + index : start + index + 1, :]
                row = jnp.concatenate([row, jnp.zeros((1, LANES - bearings), jnp.int32)], axis=1)
                total = total + pltpu.roll(row, index * bearings, 1)
            parts.append(total)
        return jnp.concatenate(parts, axis=1)

    half_columns = column_total // 2

    def scatter(*sums):
        for index, start in enumerate(range(0, steps, group)):
            ids = ids_of(start)
            value = powers[start * bearings : (start + group) * bearings, :]
            high = value.astype(jnp.bfloat16)
            low = (value - high.astype(jnp.float32)).astype(jnp.bfloat16)
            both = jnp.concatenate([high, low], axis=1)
            for unit in range(2):
                pltpu.matmul_push_rhs(both, index % 2, unit)
            for unit in range(2):
                column = lax.broadcasted_iota(jnp.int32, (half_columns, TILE), 0) + unit * half_columns
                chosen = (column == ids).astype(jnp.bfloat16)
                pltpu.matmul_acc_lhs(sums[unit], chosen, load_staged_rhs=index % 2)
        for unit in range(2):
            total = pltpu.matmul_pop(sums[unit])
            grid_ref[unit * half_columns : (unit + 1) * half_columns, :] = total[:, :LANES] + total[:, LANES:]

    pl.run_scoped(scatter, *[pltpu.ACC(unit)((half_columns, TILE), jnp.float32) for unit in range(2)])


def finish(scale, parts_ref, out_ref):
    total = jnp.sum(parts_ref[...].astype(jnp.float32), axis=0) * jnp.float32(scale)
    row = lax.broadcasted_iota(jnp.int32, (LANES, LANES), 0)
    column = lax.broadcasted_iota(jnp.int32, (LANES, LANES), 1)
    groups = LANES // BAND_CELLS
    place = (row % BAND_CELLS) * groups + row // BAND_CELLS
    order = (place == column).astype(jnp.bfloat16)
    rows = total.shape[0]
    parts = []
    for _ in range(3):
        part = total.astype(jnp.bfloat16)
        total = total - part.astype(jnp.float32)
        parts.append(part.astype(jnp.float32))
    parts = jnp.concatenate(parts, axis=0).astype(jnp.bfloat16)
    placed = jnp.dot(parts, order, preferred_element_type=jnp.float32)
    out_ref[...] = placed[:rows] + (placed[rows : 2 * rows] + placed[2 * rows :])


def on_device(starter, propagator, wavenumber, sediment_loss, env_speed, bottom, track_column):
    bearings_here, steps = track_column.shape
    columns_here, depth_cells = env_speed.shape
    bands = depth_cells // BAND_CELLS
    owners = lax.axis_size("bearing")
    freqs = lax.axis_size("freq")
    devices = owners * freqs
    column_total = columns_here * owners
    pieces = depth_cells // LANES
    smem = pl.BlockSpec(memory_space=pltpu.SMEM)
    vmem = pl.BlockSpec(memory_space=pltpu.VMEM)

    own = pl.pallas_call(
        pack,
        out_shape=jax.ShapeDtypeStruct((columns_here * pieces + EXTRA_ROWS, LANES), jnp.bfloat16),
        in_specs=[vmem] * 2,
        out_specs=vmem,
        scratch_shapes=[pltpu.VMEM((columns_here * pieces, LANES), jnp.float32)],
        name="pack",
    )(env_speed, bottom.reshape(1, -1))

    odd = [offset for offset in range(owners) if parity(offset)]
    even = [offset for offset in range(owners) if not parity(offset)]
    odd[-2:] = odd[:-3:-1]
    turns = list(zip(odd, even))
    received = []
    for turn in turns:
        pairs = [
            (bearing * freqs + freq, (bearing ^ turn[freq % 2]) * freqs + freq)
            for bearing in range(owners)
            for freq in range(freqs)
            if turn[freq % 2]
        ]
        received.append(lax.ppermute(own, ("bearing", "freq"), pairs))
    spread_out = pl.pallas_call(
        spread,
        out_shape=jax.ShapeDtypeStruct((pieces, 2 * depth_cells, LANES), jnp.bfloat16),
        in_specs=[pl.BlockSpec(memory_space=pl.ANY)],
        out_specs=vmem,
        scratch_shapes=[pltpu.SemaphoreType.DMA((pieces,))],
        compiler_params=pltpu.CompilerParams(vmem_limit_bytes=SPREAD_LIMIT),
        cost_estimate=pl.CostEstimate(flops=0, bytes_accessed=2 * propagator.size * 2, transcendentals=0),
        name="spread",
    )(propagator[0].reshape(2 * depth_cells, depth_cells))
    direct = jnp.concatenate(received, axis=0)
    direct, spread_out = lax.optimization_barrier((direct, spread_out))
    passed = lax.ppermute(direct, "freq", [(freq, freq ^ 1) for freq in range(freqs)])

    tracks = track_column.T
    grid = pl.pallas_call(
        functools.partial(propagate, turns),
        out_shape=jax.ShapeDtypeStruct((column_total, bands), jnp.float32),
        in_specs=[smem] * 3 + [vmem] * 6,
        out_specs=vmem,
        scratch_shapes=[
            pltpu.VMEM((owners * columns_here * pieces, LANES), jnp.float32),
            pltpu.VMEM((owners * columns_here * pieces, LANES), jnp.float32),
            pltpu.VMEM((columns_here, LANES), jnp.float32),
        ]
        + [pltpu.VMEM((2 * bearings_here, 2 * depth_cells), jnp.bfloat16)] * 2
        + [pltpu.VMEM((bearings_here * (pieces + 1), LANES), jnp.float32)] * 4
        + [pltpu.VMEM((steps * bearings_here, bands), jnp.float32)],
        compiler_params=pltpu.CompilerParams(vmem_limit_bytes=VMEM_LIMIT),
        name="propagate",
    )(
        tracks, wavenumber, sediment_loss, tracks, starter[0].reshape(2 * bearings_here, depth_cells),
        spread_out, own, direct, passed,
    )
    parts = lax.all_to_all(
        grid.reshape(devices, column_total // devices, bands), ("bearing", "freq"), 0, 0
    )
    scale = column_total / (bearings_here * owners * steps * freqs)
    return pl.pallas_call(
        functools.partial(finish, scale),
        out_shape=jax.ShapeDtypeStruct((column_total // devices, bands), jnp.float32),
        in_specs=[vmem],
        out_specs=vmem,
        name="finish",
    )(parts)


def solution(mesh):
    in_specs = (
        P("freq", None, "bearing", None),
        P("freq", None, None, None),
        P("freq"),
        P("freq"),
        P("bearing", None),
        P("bearing"),
        P("bearing", None),
    )
    out_specs = P(("bearing", "freq"), None)
    mapped = jax.shard_map(
        on_device, mesh=mesh, in_specs=in_specs, out_specs=out_specs, check_vma=False
    )

    def program(*arrays):
        with jax.sharding.use_abstract_mesh(mesh.abstract_mesh):
            return mapped(*arrays)

    return program
```

```python
import functools

import jax
import jax.numpy as jnp
from jax import lax
from jax.experimental import pallas as pl
from jax.experimental.pallas import tpu as pltpu
from jax.sharding import PartitionSpec as P

BAND_CELLS = 8
LANES = 128
TILE = 256
PAD_ROWS = 64
EXTRA_ROWS = 16
CODE_BASE = 256
HALF_TURN = 0.3183098861837907
SIN_TERMS = (3.141592640130706, -5.167710083507879, 2.550077523214355, -0.598291285618806, 0.07765766030210168)
COS_TERMS = (0.9999999532476083, -4.9347928306196405, 4.058411352862505, -1.3318765680803568, 0.2196896110969353)
TOGETHER = (8, 4, 2)
VMEM_LIMIT = 24 * 1024 * 1024
SPREAD_LIMIT = 24 * 1024 * 1024


def polynomial(terms, square):
    total = jnp.float32(terms[-1])
    for term in terms[-2::-1]:
        total = total * square + jnp.float32(term)
    return total


def sine_and_cosine(turns):
    nearest = jnp.round(turns)
    rest = turns - nearest
    square = rest * rest
    sine = polynomial(SIN_TERMS, square) * rest
    cosine = polynomial(COS_TERMS, square)
    return sine, cosine, (nearest.astype(jnp.int32) & 1) != 0


def pack(env_ref, bottom_ref, out_ref, wide):
    columns, depth_cells = env_ref.shape
    pieces = depth_cells // LANES
    for piece in range(pieces):
        block = env_ref[:, piece * LANES : (piece + 1) * LANES].astype(jnp.float32)
        wide[pl.ds(piece, columns, stride=pieces), :] = block
    rows = columns * pieces
    out_ref[:rows, :] = wide[...].astype(jnp.bfloat16)
    bottom = jnp.concatenate([bottom_ref[...], jnp.zeros((1, LANES - columns), jnp.int32)], axis=1)
    row = lax.broadcasted_iota(jnp.int32, (EXTRA_ROWS, LANES), 0)
    high = lax.shift_right_logical(bottom, 8)
    extra = jnp.where(row == 0, high, jnp.where(row == 1, bottom & (CODE_BASE - 1), 0))
    out_ref[rows:, :] = extra.astype(jnp.float32).astype(jnp.bfloat16)


def spread(prop_ref, out_ref, sems):
    loads = [
        pltpu.make_async_copy(
            prop_ref.at[:, piece * LANES : (piece + 1) * LANES], out_ref.at[piece], sems.at[piece]
        )
        for piece in range(out_ref.shape[0])
    ]
    for load in loads:
        load.start()
    for load in loads:
        load.wait()


def propagate(
    turns,
    track_smem, wavenumber_smem, loss_smem, tracks_ref, starter_ref, prop, own_ref, direct_ref, passed_ref,
    grid_ref, sin_table, cos_table, bottom_rows,
    field_a, field_b, sin_a, cos_a, sin_b, cos_b, powers,
):
    pieces, double_depth, _ = prop.shape
    depth_cells = double_depth // 2
    steps, bearings = track_smem.shape
    column_total = grid_ref.shape[0]
    block_rows = own_ref.shape[0]
    cell_rows = block_rows - EXTRA_ROWS
    columns_here = cell_rows // pieces
    rounds = direct_ref.shape[0] // block_rows
    stride = pieces + 1
    per_turn = wavenumber_smem[0] * jnp.float32(HALF_TURN)
    decay = jnp.exp(jnp.full((pieces, LANES), -loss_smem[0], jnp.float32))
    me = lax.axis_index("bearing")
    core = lax.axis_index("freq") % 2

    def place_of(turn, unit):
        offset = jnp.int32(0)
        for index, pair in enumerate(turns):
            offset = jnp.where(turn == index, jnp.where(unit == 0, pair[0], pair[1]), offset)
        return me ^ offset

    depth_index = lax.broadcasted_iota(jnp.int32, (pieces, LANES), 0) * LANES + lax.broadcasted_iota(
        jnp.int32, (pieces, LANES), 1
    )
    depth_index = depth_index.astype(jnp.float32)

    def tabulate(ref, place, start):
        base = place * cell_rows
        codes = ref[pl.ds(start + cell_rows, EXTRA_ROWS), :].astype(jnp.float32)
        bottoms = codes[0:1] * jnp.float32(CODE_BASE) + codes[1:2]
        own_lane = lax.broadcasted_iota(jnp.int32, (columns_here, LANES), 0) == lax.broadcasted_iota(
            jnp.int32, (columns_here, LANES), 1
        )
        bottoms = jnp.sum(jnp.where(own_lane, bottoms, jnp.float32(0)), axis=1, keepdims=True)
        bottom_rows[...] = jnp.broadcast_to(bottoms, (columns_here, LANES))
        for pair in range(columns_here // 2):
            both = ref[pl.ds(pl.multiple_of(start + pair * 2 * pieces, 2 * pieces), 2 * pieces), :]
            both = both.astype(jnp.float32) * per_turn
            for column in (2 * pair, 2 * pair + 1):
                inner = (column - 2 * pair) * pieces
                sine, cosine, minus = sine_and_cosine(both[inner : inner + pieces])
                bottom = bottom_rows[column : column + 1, :]
                damping = jnp.where(depth_index >= bottom, decay, jnp.float32(1.0))
                rows = pl.ds(pl.multiple_of(base + column * pieces, pieces), pieces)
                damping = jnp.where(minus, -damping, damping)
                sin_table[rows, :] = sine * damping
                cos_table[rows, :] = cosine * damping

    for index, ref in enumerate((direct_ref, passed_ref)):

        def one(turn, carry, ref=ref, index=index):
            place = place_of(turn, core ^ index)

            @pl.when(place != me)
            def _():
                tabulate(ref, place, turn * block_rows)

            return carry

        lax.fori_loop(0, rounds, one, 0)

    def put(field, cells, real, imaginary):
        beyond = slice(depth_cells + cells.start, depth_cells + cells.stop)
        field[:bearings, cells] = real
        field[:bearings, beyond] = -imaginary
        field[bearings:, cells] = imaginary
        field[bearings:, beyond] = real

    put(field_a, slice(0, depth_cells), starter_ref[:bearings, :], starter_ref[bearings:, :])

    def prepare(step, sin_ref, cos_ref, which):
        for bearing in which:
            column = track_smem[step, bearing]
            rows = pl.ds(pl.multiple_of(column * pieces, pieces), pieces)
            sin_ref[bearing * stride : bearing * stride + pieces, :] = sin_table[rows, :]
            cos_ref[bearing * stride : bearing * stride + pieces, :] = cos_table[rows, :]

    lane = lax.broadcasted_iota(jnp.int32, (bearings, LANES), 1)

    def fold(first, second, width):
        return jnp.where(
            (lane & width) == 0,
            first + pltpu.roll(first, LANES - width, 1),
            second + pltpu.roll(second, width, 1),
        )

    tiles = depth_cells // TILE
    halves = tiles // 2
    pieces_in = 2 * TILE // LANES
    early = [tile + part * tiles for tile in range(tiles - 2) for part in range(2)]
    late = [tile + part * tiles for tile in range(tiles - 2, tiles) for part in range(2)]
    slots_of_step = halves * (len(early) + len(late))
    nothing = jnp.zeros((PAD_ROWS, TILE), jnp.bfloat16)

    def run(*accumulators):
        sums, spare = accumulators[: 2 * halves], accumulators[2 * halves :]
        count = [0]

        def multiply(field, half, tile):
            register = count[0] % 2
            count[0] += 1
            cells = slice(tile * TILE, (tile + 1) * TILE)
            for unit in range(2):
                first = (2 * half + unit) * (TILE // LANES)
                weights = jnp.concatenate([prop[first, cells, :], prop[first + 1, cells, :]], axis=1)
                pltpu.matmul_push_rhs(weights, register, unit)
            for unit in range(2):
                pltpu.matmul_acc_lhs(sums[2 * half + unit], field[:, cells], load_staged_rhs=register)
                pltpu.matmul_acc_lhs(spare[unit], nothing)

        def begin(field):
            for half in range(halves):
                for tile in early:
                    multiply(field, half, tile)

        def advance(step, field, following, sin_ref, cos_ref, next_sin, next_cos, last=False):
            work = [[] for _ in range(slots_of_step + 1)]
            share = -(-bearings // slots_of_step)
            for slot in range(0 if last else slots_of_step):
                which = range(slot * share, min(bearings, (slot + 1) * share))
                work[slot].append(functools.partial(prepare, step + 1, next_sin, next_cos, which))
            moved = {}
            folded = {}

            def pop(half):
                for unit in range(2):
                    moved[2 * half + unit] = pltpu.matmul_pop(sums[2 * half + unit])

            def screen(piece):
                value = moved[piece * LANES // TILE]
                inner = slice(piece * LANES % TILE, piece * LANES % TILE + LANES)
                moved_re = value[:bearings, inner]
                moved_im = value[bearings:, inner]
                sine = sin_ref[pl.ds(piece, bearings, stride=stride), :]
                cosine = cos_ref[pl.ds(piece, bearings, stride=stride), :]
                screened_re = moved_re * cosine - moved_im * sine
                screened_im = moved_re * sine + moved_im * cosine
                outer = slice(piece * LANES, (piece + 1) * LANES)
                put(following, outer, screened_re.astype(jnp.bfloat16), screened_im.astype(jnp.bfloat16))
                level, value = 1, screened_re * screened_re + screened_im * screened_im
                at = piece
                while at % 2 == 1:
                    value = fold(folded.pop((level, at - 1)), value, level)
                    at //= 2
                    level *= 2
                folded[level, at] = value

            for half in range(halves):
                after = (half + 1) * len(late)
                work[after].append(functools.partial(pop, half))
                for index in range(pieces_in):
                    slot = after + 1 + index
                    if half < halves - 1:
                        slot = min(slot, after + len(late) - 1)
                    work[min(slot, slots_of_step)].append(functools.partial(screen, half * pieces_in + index))
            slot = 0
            for source, order in ((field, late), (following, early)):
                for half in range(halves):
                    for tile in order:
                        if source is field or not last:
                            multiply(source, half, tile)
                        for item in work[slot]:
                            item()
                        slot += 1
            for item in work[slot]:
                item()
            rows = pl.ds(pl.multiple_of(step * bearings, bearings), bearings)
            powers[rows, :] = folded[pieces, 0]

        begin(field_a)
        tabulate(own_ref, me, 0)
        prepare(0, sin_a, cos_a, range(bearings))

        together = next(number for number in TOGETHER if steps % number == 0)

        def some_steps(index, carry, last=False):
            for step in range(0, together, 2):
                advance(index * together + step, field_a, field_b, sin_a, cos_a, sin_b, cos_b)
                ends = last and step + 2 == together
                advance(index * together + step + 1, field_b, field_a, sin_b, cos_b, sin_a, cos_a, ends)
            return carry

        lax.fori_loop(0, steps // together - 1, some_steps, 0)
        some_steps(steps // together - 1, 0, True)
        for accumulator in spare:
            pltpu.matmul_pop(accumulator)

    pl.run_scoped(
        run,
        *[pltpu.ACC(unit % 2)((2 * bearings, TILE), jnp.float32) for unit in range(2 * halves)],
        *[pltpu.ACC(unit)((PAD_ROWS, TILE), jnp.float32) for unit in range(2)],
    )

    group = TILE // bearings
    lanes_of_row = lax.broadcasted_iota(jnp.int32, (1, LANES), 1)

    def ids_of(first):
        parts = []
        for start in range(first, first + group, LANES // bearings):
            row = tracks_ref[start : start + 1, :]
            total = jnp.concatenate([row, jnp.zeros((1, LANES - bearings), jnp.int32)], axis=1)
            for index in range(1, LANES // bearings):
                row = tracks_ref[start + index : start + index + 1, :]
                row = jnp.concatenate([row, jnp.zeros((1, LANES - bearings), jnp.int32)], axis=1)
                total = total + pltpu.roll(row, index * bearings, 1)
            parts.append(total)
        return jnp.concatenate(parts, axis=1)

    half_columns = column_total // 2

    def scatter(*sums):
        for index, start in enumerate(range(0, steps, group)):
            ids = ids_of(start)
            value = powers[start * bearings : (start + group) * bearings, :]
            high = value.astype(jnp.bfloat16)
            low = (value - high.astype(jnp.float32)).astype(jnp.bfloat16)
            both = jnp.concatenate([high, low], axis=1)
            for unit in range(2):
                pltpu.matmul_push_rhs(both, index % 2, unit)
            for unit in range(2):
                column = lax.broadcasted_iota(jnp.int32, (half_columns, TILE), 0) + unit * half_columns
                chosen = (column == ids).astype(jnp.bfloat16)
                pltpu.matmul_acc_lhs(sums[unit], chosen, load_staged_rhs=index % 2)
        for unit in range(2):
            total = pltpu.matmul_pop(sums[unit])
            grid_ref[unit * half_columns : (unit + 1) * half_columns, :] = total[:, :LANES] + total[:, LANES:]

    pl.run_scoped(scatter, *[pltpu.ACC(unit)((half_columns, TILE), jnp.float32) for unit in range(2)])


def finish(scale, parts_ref, out_ref):
    total = jnp.sum(parts_ref[...].astype(jnp.float32), axis=0) * jnp.float32(scale)
    row = lax.broadcasted_iota(jnp.int32, (LANES, LANES), 0)
    column = lax.broadcasted_iota(jnp.int32, (LANES, LANES), 1)
    groups = LANES // BAND_CELLS
    place = (row % BAND_CELLS) * groups + row // BAND_CELLS
    order = (place == column).astype(jnp.bfloat16)
    rows = total.shape[0]
    parts = []
    for _ in range(3):
        part = total.astype(jnp.bfloat16)
        total = total - part.astype(jnp.float32)
        parts.append(part.astype(jnp.float32))
    parts = jnp.concatenate(parts, axis=0).astype(jnp.bfloat16)
    placed = jnp.dot(parts, order, preferred_element_type=jnp.float32)
    out_ref[...] = placed[:rows] + (placed[rows : 2 * rows] + placed[2 * rows :])


def on_device(starter, propagator, wavenumber, sediment_loss, env_speed, bottom, track_column):
    bearings_here, steps = track_column.shape
    columns_here, depth_cells = env_speed.shape
    bands = depth_cells // BAND_CELLS
    owners = lax.axis_size("bearing")
    freqs = lax.axis_size("freq")
    devices = owners * freqs
    column_total = columns_here * owners
    pieces = depth_cells // LANES
    smem = pl.BlockSpec(memory_space=pltpu.SMEM)
    vmem = pl.BlockSpec(memory_space=pltpu.VMEM)

    own = pl.pallas_call(
        pack,
        out_shape=jax.ShapeDtypeStruct((columns_here * pieces + EXTRA_ROWS, LANES), jnp.bfloat16),
        in_specs=[vmem] * 2,
        out_specs=vmem,
        scratch_shapes=[pltpu.VMEM((columns_here * pieces, LANES), jnp.float32)],
        name="pack",
    )(env_speed, bottom.reshape(1, -1))

    middle = owners // 2
    near = [*range(2, middle), middle, 1]
    far = [*range(middle + 1, owners), 0]
    turns = list(zip(near, far))[::-1]
    received = []
    for turn in turns:
        pairs = [
            (bearing * freqs + freq, (bearing ^ turn[freq % 2]) * freqs + freq)
            for bearing in range(owners)
            for freq in range(freqs)
            if turn[freq % 2]
        ]
        received.append(lax.ppermute(own, ("bearing", "freq"), pairs))
    spread_out = pl.pallas_call(
        spread,
        out_shape=jax.ShapeDtypeStruct((pieces, 2 * depth_cells, LANES), jnp.bfloat16),
        in_specs=[pl.BlockSpec(memory_space=pl.ANY)],
        out_specs=vmem,
        scratch_shapes=[pltpu.SemaphoreType.DMA((pieces,))],
        compiler_params=pltpu.CompilerParams(vmem_limit_bytes=SPREAD_LIMIT),
        cost_estimate=pl.CostEstimate(flops=0, bytes_accessed=2 * propagator.size * 2, transcendentals=0),
        name="spread",
    )(propagator[0].reshape(2 * depth_cells, depth_cells))
    direct = jnp.concatenate(received, axis=0)
    direct, spread_out = lax.optimization_barrier((direct, spread_out))
    passed = lax.ppermute(direct, "freq", [(freq, freq ^ 1) for freq in range(freqs)])

    tracks = track_column.T
    grid = pl.pallas_call(
        functools.partial(propagate, turns),
        out_shape=jax.ShapeDtypeStruct((column_total, bands), jnp.float32),
        in_specs=[smem] * 3 + [vmem] * 6,
        out_specs=vmem,
        scratch_shapes=[
            pltpu.VMEM((owners * columns_here * pieces, LANES), jnp.float32),
            pltpu.VMEM((owners * columns_here * pieces, LANES), jnp.float32),
            pltpu.VMEM((columns_here, LANES), jnp.float32),
        ]
        + [pltpu.VMEM((2 * bearings_here, 2 * depth_cells), jnp.bfloat16)] * 2
        + [pltpu.VMEM((bearings_here * (pieces + 1), LANES), jnp.float32)] * 4
        + [pltpu.VMEM((steps * bearings_here, bands), jnp.float32)],
        compiler_params=pltpu.CompilerParams(vmem_limit_bytes=VMEM_LIMIT),
        name="propagate",
    )(
        tracks, wavenumber, sediment_loss, tracks, starter[0].reshape(2 * bearings_here, depth_cells),
        spread_out, own, direct, passed,
    )
    parts = lax.all_to_all(
        grid.reshape(devices, column_total // devices, bands), ("bearing", "freq"), 0, 0
    )
    scale = column_total / (bearings_here * owners * steps * freqs)
    return pl.pallas_call(
        functools.partial(finish, scale),
        out_shape=jax.ShapeDtypeStruct((column_total // devices, bands), jnp.float32),
        in_specs=[vmem],
        out_specs=vmem,
        name="finish",
    )(parts)


def solution(mesh):
    in_specs = (
        P("freq", None, "bearing", None),
        P("freq", None, None, None),
        P("freq"),
        P("freq"),
        P("bearing", None),
        P("bearing"),
        P("bearing", None),
    )
    out_specs = P(("bearing", "freq"), None)
    mapped = jax.shard_map(
        on_device, mesh=mesh, in_specs=in_specs, out_specs=out_specs, check_vma=False
    )

    def program(*arrays):
        with jax.sharding.use_abstract_mesh(mesh.abstract_mesh):
            return mapped(*arrays)

    return program
```

```python
import functools

import jax
import jax.numpy as jnp
from jax import lax
from jax.experimental import pallas as pl
from jax.experimental.pallas import tpu as pltpu
from jax.sharding import PartitionSpec as P

BAND_CELLS = 8
LANES = 128
TILE = 256
PAD_ROWS = 64
EXTRA_ROWS = 16
CODE_BASE = 256
HALF_TURN = 0.3183098861837907
SIN_TERMS = (3.141592640130706, -5.167710083507879, 2.550077523214355, -0.598291285618806, 0.07765766030210168)
COS_TERMS = (0.9999999532476083, -4.9347928306196405, 4.058411352862505, -1.3318765680803568, 0.2196896110969353)
TOGETHER = (8, 4, 2)
VMEM_LIMIT = 24 * 1024 * 1024
SPREAD_LIMIT = 24 * 1024 * 1024


def polynomial(terms, square):
    total = jnp.float32(terms[-1])
    for term in terms[-2::-1]:
        total = total * square + jnp.float32(term)
    return total


def sine_and_cosine(turns):
    nearest = jnp.round(turns)
    rest = turns - nearest
    square = rest * rest
    sine = polynomial(SIN_TERMS, square) * rest
    cosine = polynomial(COS_TERMS, square)
    return sine, cosine, (nearest.astype(jnp.int32) & 1) != 0


def pack(env_ref, bottom_ref, out_ref, wide):
    columns, depth_cells = env_ref.shape
    pieces = depth_cells // LANES
    for piece in range(pieces):
        block = env_ref[:, piece * LANES : (piece + 1) * LANES].astype(jnp.float32)
        wide[pl.ds(piece, columns, stride=pieces), :] = block
    rows = columns * pieces
    out_ref[:rows, :] = wide[...].astype(jnp.bfloat16)
    bottom = jnp.concatenate([bottom_ref[...], jnp.zeros((1, LANES - columns), jnp.int32)], axis=1)
    row = lax.broadcasted_iota(jnp.int32, (EXTRA_ROWS, LANES), 0)
    high = lax.shift_right_logical(bottom, 8)
    extra = jnp.where(row == 0, high, jnp.where(row == 1, bottom & (CODE_BASE - 1), 0))
    out_ref[rows:, :] = extra.astype(jnp.float32).astype(jnp.bfloat16)


def spread(prop_ref, out_ref, sems):
    loads = [
        pltpu.make_async_copy(
            prop_ref.at[:, piece * LANES : (piece + 1) * LANES], out_ref.at[piece], sems.at[piece]
        )
        for piece in range(out_ref.shape[0])
    ]
    for load in loads:
        load.start()
    for load in loads:
        load.wait()


def propagate(
    turns,
    track_smem, wavenumber_smem, loss_smem, tracks_ref, starter_ref, prop, own_ref, direct_ref, passed_ref,
    grid_ref, sin_table, cos_table, bottom_rows,
    field_a, field_b, sin_a, cos_a, sin_b, cos_b, powers, chosen,
):
    pieces, double_depth, _ = prop.shape
    depth_cells = double_depth // 2
    steps, bearings = track_smem.shape
    column_total = grid_ref.shape[0]
    block_rows = own_ref.shape[0]
    cell_rows = block_rows - EXTRA_ROWS
    columns_here = cell_rows // pieces
    rounds = direct_ref.shape[0] // block_rows
    stride = pieces + 1
    per_turn = wavenumber_smem[0] * jnp.float32(HALF_TURN)
    decay = jnp.exp(jnp.full((pieces, LANES), -loss_smem[0], jnp.float32))
    me = lax.axis_index("bearing")
    core = lax.axis_index("freq") % 2

    def place_of(turn, unit):
        offset = jnp.int32(0)
        for index, pair in enumerate(turns):
            offset = jnp.where(turn == index, jnp.where(unit == 0, pair[0], pair[1]), offset)
        return me ^ offset

    depth_index = lax.broadcasted_iota(jnp.int32, (pieces, LANES), 0) * LANES + lax.broadcasted_iota(
        jnp.int32, (pieces, LANES), 1
    )
    depth_index = depth_index.astype(jnp.float32)

    def tabulate(ref, place, start):
        base = place * cell_rows
        codes = ref[pl.ds(start + cell_rows, EXTRA_ROWS), :].astype(jnp.float32)
        bottoms = codes[0:1] * jnp.float32(CODE_BASE) + codes[1:2]
        own_lane = lax.broadcasted_iota(jnp.int32, (columns_here, LANES), 0) == lax.broadcasted_iota(
            jnp.int32, (columns_here, LANES), 1
        )
        bottoms = jnp.sum(jnp.where(own_lane, bottoms, jnp.float32(0)), axis=1, keepdims=True)
        bottom_rows[...] = jnp.broadcast_to(bottoms, (columns_here, LANES))
        for pair in range(columns_here // 2):
            both = ref[pl.ds(pl.multiple_of(start + pair * 2 * pieces, 2 * pieces), 2 * pieces), :]
            both = both.astype(jnp.float32) * per_turn
            for column in (2 * pair, 2 * pair + 1):
                inner = (column - 2 * pair) * pieces
                sine, cosine, minus = sine_and_cosine(both[inner : inner + pieces])
                bottom = bottom_rows[column : column + 1, :]
                damping = jnp.where(depth_index >= bottom, decay, jnp.float32(1.0))
                rows = pl.ds(pl.multiple_of(base + column * pieces, pieces), pieces)
                damping = jnp.where(minus, -damping, damping)
                sin_table[rows, :] = sine * damping
                cos_table[rows, :] = cosine * damping

    for index, ref in enumerate((direct_ref, passed_ref)):

        def one(turn, carry, ref=ref, index=index):
            place = place_of(turn, core ^ index)

            @pl.when(place != me)
            def _():
                tabulate(ref, place, turn * block_rows)

            return carry

        lax.fori_loop(0, rounds, one, 0)

    def put(field, cells, real, imaginary):
        beyond = slice(depth_cells + cells.start, depth_cells + cells.stop)
        field[:bearings, cells] = real
        field[:bearings, beyond] = -imaginary
        field[bearings:, cells] = imaginary
        field[bearings:, beyond] = real

    put(field_a, slice(0, depth_cells), starter_ref[:bearings, :], starter_ref[bearings:, :])

    def prepare(step, sin_ref, cos_ref, which):
        for bearing in which:
            column = track_smem[step, bearing]
            rows = pl.ds(pl.multiple_of(column * pieces, pieces), pieces)
            sin_ref[bearing * stride : bearing * stride + pieces, :] = sin_table[rows, :]
            cos_ref[bearing * stride : bearing * stride + pieces, :] = cos_table[rows, :]

    lane = lax.broadcasted_iota(jnp.int32, (bearings, LANES), 1)

    def fold(first, second, width):
        return jnp.where(
            (lane & width) == 0,
            first + pltpu.roll(first, LANES - width, 1),
            second + pltpu.roll(second, width, 1),
        )

    tiles = depth_cells // TILE
    halves = tiles // 2
    pieces_in = 2 * TILE // LANES
    early = [tile + part * tiles for tile in range(tiles - 2) for part in range(2)]
    late = [tile + part * tiles for tile in range(tiles - 2, tiles) for part in range(2)]
    slots_of_step = halves * (len(early) + len(late))
    nothing = jnp.zeros((PAD_ROWS, TILE), jnp.bfloat16)

    group = TILE // bearings
    lanes_of_row = lax.broadcasted_iota(jnp.int32, (1, LANES), 1)

    def ids_of(first):
        parts = []
        for start in range(first, first + group, LANES // bearings):
            row = tracks_ref[start : start + 1, :]
            total = jnp.concatenate([row, jnp.zeros((1, LANES - bearings), jnp.int32)], axis=1)
            for index in range(1, LANES // bearings):
                row = tracks_ref[start + index : start + index + 1, :]
                row = jnp.concatenate([row, jnp.zeros((1, LANES - bearings), jnp.int32)], axis=1)
                total = total + pltpu.roll(row, index * bearings, 1)
            parts.append(total)
        return jnp.concatenate(parts, axis=1)

    def choose():
        column = lax.broadcasted_iota(jnp.int32, (column_total, TILE), 0)
        for index, start in enumerate(range(0, steps, group)):
            chosen[:, index * TILE : (index + 1) * TILE] = (column == ids_of(start)).astype(jnp.bfloat16)

    def run(*accumulators):
        sums, spare = accumulators[: 2 * halves], accumulators[2 * halves :]
        count = [0]

        def multiply(field, half, tile):
            register = count[0] % 2
            count[0] += 1
            cells = slice(tile * TILE, (tile + 1) * TILE)
            for unit in range(2):
                first = (2 * half + unit) * (TILE // LANES)
                weights = jnp.concatenate([prop[first, cells, :], prop[first + 1, cells, :]], axis=1)
                pltpu.matmul_push_rhs(weights, register, unit)
            for unit in range(2):
                pltpu.matmul_acc_lhs(sums[2 * half + unit], field[:, cells], load_staged_rhs=register)
                pltpu.matmul_acc_lhs(spare[unit], nothing)

        def begin(field):
            for half in range(halves):
                for tile in early:
                    multiply(field, half, tile)

        def advance(step, field, following, sin_ref, cos_ref, next_sin, next_cos, last=False):
            work = [[] for _ in range(slots_of_step + 1)]
            share = -(-bearings // slots_of_step)
            for slot in range(0 if last else slots_of_step):
                which = range(slot * share, min(bearings, (slot + 1) * share))
                work[slot].append(functools.partial(prepare, step + 1, next_sin, next_cos, which))
            moved = {}
            folded = {}

            def pop(half):
                for unit in range(2):
                    moved[2 * half + unit] = pltpu.matmul_pop(sums[2 * half + unit])

            def screen(piece):
                value = moved[piece * LANES // TILE]
                inner = slice(piece * LANES % TILE, piece * LANES % TILE + LANES)
                moved_re = value[:bearings, inner]
                moved_im = value[bearings:, inner]
                sine = sin_ref[pl.ds(piece, bearings, stride=stride), :]
                cosine = cos_ref[pl.ds(piece, bearings, stride=stride), :]
                screened_re = moved_re * cosine - moved_im * sine
                screened_im = moved_re * sine + moved_im * cosine
                outer = slice(piece * LANES, (piece + 1) * LANES)
                put(following, outer, screened_re.astype(jnp.bfloat16), screened_im.astype(jnp.bfloat16))
                level, value = 1, screened_re * screened_re + screened_im * screened_im
                at = piece
                while at % 2 == 1:
                    value = fold(folded.pop((level, at - 1)), value, level)
                    at //= 2
                    level *= 2
                folded[level, at] = value

            for half in range(halves):
                after = (half + 1) * len(late)
                work[after].append(functools.partial(pop, half))
                for index in range(pieces_in):
                    slot = after + 1 + index
                    if half < halves - 1:
                        slot = min(slot, after + len(late) - 1)
                    work[min(slot, slots_of_step)].append(functools.partial(screen, half * pieces_in + index))
            slot = 0
            for source, order in ((field, late), (following, early)):
                for half in range(halves):
                    for tile in order:
                        if source is field or not last:
                            multiply(source, half, tile)
                        for item in work[slot]:
                            item()
                        slot += 1
            for item in work[slot]:
                item()
            rows = pl.ds(pl.multiple_of(step * bearings, bearings), bearings)
            powers[rows, :] = folded[pieces, 0]

        begin(field_a)
        tabulate(own_ref, me, 0)
        prepare(0, sin_a, cos_a, range(bearings))

        together = next(number for number in TOGETHER if steps % number == 0)

        def some_steps(index, carry, last=False):
            for step in range(0, together, 2):
                advance(index * together + step, field_a, field_b, sin_a, cos_a, sin_b, cos_b)
                ends = last and step + 2 == together
                advance(index * together + step + 1, field_b, field_a, sin_b, cos_b, sin_a, cos_a, ends)
            return carry

        lax.fori_loop(0, steps // together - 1, some_steps, 0)
        choose()
        some_steps(steps // together - 1, 0, True)
        for accumulator in spare:
            pltpu.matmul_pop(accumulator)

    pl.run_scoped(
        run,
        *[pltpu.ACC(unit % 2)((2 * bearings, TILE), jnp.float32) for unit in range(2 * halves)],
        *[pltpu.ACC(unit)((PAD_ROWS, TILE), jnp.float32) for unit in range(2)],
    )

    half_columns = column_total // 2

    def scatter(*sums):
        for index, start in enumerate(range(0, steps, group)):
            value = powers[start * bearings : (start + group) * bearings, :]
            high = value.astype(jnp.bfloat16)
            low = (value - high.astype(jnp.float32)).astype(jnp.bfloat16)
            both = jnp.concatenate([high, low], axis=1)
            for unit in range(2):
                pltpu.matmul_push_rhs(both, index % 2, unit)
            for unit in range(2):
                rows = slice(unit * half_columns, (unit + 1) * half_columns)
                cells = slice(index * TILE, (index + 1) * TILE)
                pltpu.matmul_acc_lhs(sums[unit], chosen[rows, cells], load_staged_rhs=index % 2)
        for unit in range(2):
            total = pltpu.matmul_pop(sums[unit])
            grid_ref[unit * half_columns : (unit + 1) * half_columns, :] = total[:, :LANES] + total[:, LANES:]

    pl.run_scoped(scatter, *[pltpu.ACC(unit)((half_columns, TILE), jnp.float32) for unit in range(2)])


def finish(scale, parts_ref, out_ref):
    total = jnp.sum(parts_ref[...].astype(jnp.float32), axis=0) * jnp.float32(scale)
    row = lax.broadcasted_iota(jnp.int32, (LANES, LANES), 0)
    column = lax.broadcasted_iota(jnp.int32, (LANES, LANES), 1)
    groups = LANES // BAND_CELLS
    place = (row % BAND_CELLS) * groups + row // BAND_CELLS
    order = (place == column).astype(jnp.bfloat16)
    rows = total.shape[0]
    parts = []
    for _ in range(3):
        part = total.astype(jnp.bfloat16)
        total = total - part.astype(jnp.float32)
        parts.append(part.astype(jnp.float32))
    parts = jnp.concatenate(parts, axis=0).astype(jnp.bfloat16)
    placed = jnp.dot(parts, order, preferred_element_type=jnp.float32)
    out_ref[...] = placed[:rows] + (placed[rows : 2 * rows] + placed[2 * rows :])


def on_device(starter, propagator, wavenumber, sediment_loss, env_speed, bottom, track_column):
    bearings_here, steps = track_column.shape
    columns_here, depth_cells = env_speed.shape
    bands = depth_cells // BAND_CELLS
    owners = lax.axis_size("bearing")
    freqs = lax.axis_size("freq")
    devices = owners * freqs
    column_total = columns_here * owners
    pieces = depth_cells // LANES
    smem = pl.BlockSpec(memory_space=pltpu.SMEM)
    vmem = pl.BlockSpec(memory_space=pltpu.VMEM)

    own = pl.pallas_call(
        pack,
        out_shape=jax.ShapeDtypeStruct((columns_here * pieces + EXTRA_ROWS, LANES), jnp.bfloat16),
        in_specs=[vmem] * 2,
        out_specs=vmem,
        scratch_shapes=[pltpu.VMEM((columns_here * pieces, LANES), jnp.float32)],
        name="pack",
    )(env_speed, bottom.reshape(1, -1))

    middle = owners // 2
    near = [*range(2, middle), middle, 1]
    far = [*range(middle + 1, owners), 0]
    turns = list(zip(near, far))[::-1]
    received = []
    for turn in turns:
        pairs = [
            (bearing * freqs + freq, (bearing ^ turn[freq % 2]) * freqs + freq)
            for bearing in range(owners)
            for freq in range(freqs)
            if turn[freq % 2]
        ]
        received.append(lax.ppermute(own, ("bearing", "freq"), pairs))
    spread_out = pl.pallas_call(
        spread,
        out_shape=jax.ShapeDtypeStruct((pieces, 2 * depth_cells, LANES), jnp.bfloat16),
        in_specs=[pl.BlockSpec(memory_space=pl.ANY)],
        out_specs=vmem,
        scratch_shapes=[pltpu.SemaphoreType.DMA((pieces,))],
        compiler_params=pltpu.CompilerParams(vmem_limit_bytes=SPREAD_LIMIT),
        cost_estimate=pl.CostEstimate(flops=0, bytes_accessed=2 * propagator.size * 2, transcendentals=0),
        name="spread",
    )(propagator[0].reshape(2 * depth_cells, depth_cells))
    direct = jnp.concatenate(received, axis=0)
    direct, spread_out = lax.optimization_barrier((direct, spread_out))
    passed = lax.ppermute(direct, "freq", [(freq, freq ^ 1) for freq in range(freqs)])

    tracks = track_column.T
    grid = pl.pallas_call(
        functools.partial(propagate, turns),
        out_shape=jax.ShapeDtypeStruct((column_total, bands), jnp.float32),
        in_specs=[smem] * 3 + [vmem] * 6,
        out_specs=vmem,
        scratch_shapes=[
            pltpu.VMEM((owners * columns_here * pieces, LANES), jnp.float32),
            pltpu.VMEM((owners * columns_here * pieces, LANES), jnp.float32),
            pltpu.VMEM((columns_here, LANES), jnp.float32),
        ]
        + [pltpu.VMEM((2 * bearings_here, 2 * depth_cells), jnp.bfloat16)] * 2
        + [pltpu.VMEM((bearings_here * (pieces + 1), LANES), jnp.float32)] * 4
        + [pltpu.VMEM((steps * bearings_here, bands), jnp.float32)]
        + [pltpu.VMEM((column_total, steps * bearings_here), jnp.bfloat16)],
        compiler_params=pltpu.CompilerParams(vmem_limit_bytes=VMEM_LIMIT),
        name="propagate",
    )(
        tracks, wavenumber, sediment_loss, tracks, starter[0].reshape(2 * bearings_here, depth_cells),
        spread_out, own, direct, passed,
    )
    parts = lax.all_to_all(
        grid.reshape(devices, column_total // devices, bands), ("bearing", "freq"), 0, 0
    )
    scale = column_total / (bearings_here * owners * steps * freqs)
    return pl.pallas_call(
        functools.partial(finish, scale),
        out_shape=jax.ShapeDtypeStruct((column_total // devices, bands), jnp.float32),
        in_specs=[vmem],
        out_specs=vmem,
        name="finish",
    )(parts)


def solution(mesh):
    in_specs = (
        P("freq", None, "bearing", None),
        P("freq", None, None, None),
        P("freq"),
        P("freq"),
        P("bearing", None),
        P("bearing"),
        P("bearing", None),
    )
    out_specs = P(("bearing", "freq"), None)
    mapped = jax.shard_map(
        on_device, mesh=mesh, in_specs=in_specs, out_specs=out_specs, check_vma=False
    )

    def program(*arrays):
        with jax.sharding.use_abstract_mesh(mesh.abstract_mesh):
            return mapped(*arrays)

    return program
```
